512 devices in a mesh: flap: 16 (over z_lo, y), gust: 16 (over x, z_hi), span: 2 (over core).
Axes of the slice: x: 4, y: 8, z: 8 (z_hi: 4, z_lo: 2; z = z_hi * 2 + z_lo), core: 2. Of those that a mesh axis runs over, the one named last changes fastest.
Arguments:
- state: float32 [16, 16, 5, 4, 48, 128], P('flap', 'gust', None, 'span'), may hold values from -1 to 4, as said below
- frame_velocity: float32 [16, 16, 3], P('flap', 'gust'), may hold values from -3 to 3
- dtau: float32 [4, 48, 128], P('span'), may hold values from 0.02 to 0.08
- live_mask: int32 [4, 48, 128], P('span'), may hold values 0 or 1
- link: int32 [128], replicated, may hold values from 0 to 127, each once
Outputs:
- state_out: float32 [16, 16, 5, 4, 48, 128], P('flap', 'gust', None, 'span')
The draws below stay inside these ranges and needn't reach their ends.
Inputs may be any that keep to these rules, and one draw needn't show every extreme that they name: `state`: every cell holds a density of 0.7 or more, and a total energy that leaves a pressure of 0.5 or more.
All inputs are finite; a program needn't handle non-finite values. No bound on the sum of `live_mask` on one device may be relied on, other than what follows from the above.
Results may differ from the reference program's by a relative error of at most 0.0003.
Values sent between devices are 32-bit elements; how exact they have to be, the bound alone decides.
No kernel may reach another device: no remote copies, remote signals or barrier semaphores. Data moves between devices by JAX's collectives and lax.ppermute only.
A program may use at most 64 MiB of HBM per device.

```python
import math
import jax
import jax.numpy as jnp
from jax import lax

NI = 128
NJ = 48
STEPS = 2
HF = 16
HG = 16
NK = 4


def draw_state(key, part):
    key = jax.random.fold_in(key, 11)
    keys = jax.random.split(key, 3)
    shape = (HF, HG, NK, NJ, NI)
    density = jax.random.uniform(keys[0], shape, jnp.float32, 0.8, 1.2)
    noise = jnp.clip(0.1 * jax.random.normal(keys[1], (3,) + shape, jnp.float32), -0.3, 0.3)
    pressure = jax.random.uniform(keys[2], shape, jnp.float32, 0.6, 0.9)
    base = jnp.array([0.5, 0.0, 0.0], jnp.float32).reshape((3, 1, 1, 1, 1, 1))
    velocity = base + noise
    momenta = density * velocity
    energy = pressure / 0.4 + 0.5 * density * jnp.sum(velocity * velocity, axis=0)
    fields = jnp.concatenate([density[None], momenta, energy[None]], 0)
    return jnp.moveaxis(fields, 0, 2).astype(jnp.float32)


def plant(values, own_key, smallest, top_value):
    dims = values.shape
    index_at = [jax.random.randint(jax.random.fold_in(own_key, axis), (), 0, dims[axis]) for axis in range(len(dims))]
    values = values.at[tuple(index_at)].set(smallest)
    longest = dims.index(max(dims))
    index_at[longest] = (index_at[longest] + 1) % dims[longest]
    return values.at[tuple(index_at)].set(top_value)


def shard_levels(rng, shape, cuts, smallest, largest):
    gain, own = 1.0, jax.random.fold_in(rng, 6)
    for position, shards_of in cuts:
        draws = jnp.exp(jax.random.uniform(jax.random.fold_in(own, position), (shards_of,), jnp.float32, smallest / len(cuts), largest / len(cuts)))
        gain = gain * jnp.repeat(draws, shape[position] // shards_of).reshape([-1 if axis == position else 1 for axis in range(len(shape))])
    return gain


def bell_draw(key, dims, deviation, most, cuts=(), held_as=jnp.bfloat16):
    values = deviation * jax.random.normal(key, dims, jnp.float32)
    if cuts:
        values = values * shard_levels(key, dims, cuts, -0.22, 0.18)
    return jnp.clip(values, -most, most).astype(held_as)


def setup_inputs(seed: int = 0) -> dict:
    splits = jax.random.split(jax.random.key(seed), 6)
    return {
        "state": draw_state(jax.random.fold_in(splits[5], 71), 0),
        "frame_velocity": bell_draw(splits[1], (HF, HG, 3), 0.2, 3.0, ((0, 16), (1, 16)), jnp.float32),
        "dtau": jnp.clip(jnp.exp(math.log(0.08) - 1.3862944 * jax.random.uniform(splits[2], (NK, NJ, NI), jnp.float32) ** shard_levels(splits[2], (NK, NJ, NI), ((0, 2),), -0.2, 0.2)), 0.02, 0.08),
        "live_mask": plant((jax.random.randint(splits[3], (NK, NJ, NI), 0, 16) < 15).astype(jnp.int32), jax.random.fold_in(splits[3], 1), 0, 1),
        "link": jax.random.permutation(splits[4], NI).astype(jnp.int32),
    }


GAMMA = 1.4
VISC = 0.12

def instance_matrix(count, omega):
    rows = jnp.arange(count)[:, None]
    cols = jnp.arange(count)[None, :]
    offset = rows - cols
    angle = jnp.pi * offset.astype(jnp.float32) / count
    parity = jnp.where(offset % 2 == 0, 1.0, -1.0).astype(jnp.float32)
    offdiag = offset != 0
    safe = jnp.where(offdiag, angle, 0.5 * jnp.pi)
    first = jnp.where(offdiag, 0.5 * parity / jnp.tan(safe), 0.0)
    sines = jnp.sin(safe)
    second = jnp.where(offdiag, -0.5 * parity / (sines * sines), -(count * count / 12.0 + 1.0 / 6.0))
    return (omega * first - VISC * second).astype(jnp.float32)

def unit_vector(axis, ndim):
    values = jnp.array([1.0 if a == axis else 0.0 for a in range(3)], jnp.float32)
    return values.reshape((3,) + (1,) * ndim)

def primitives(state):
    density = state[0]
    velocity = state[1:4] / density
    pressure = (GAMMA - 1.0) * (state[4] - 0.5 * density * lax.optimization_barrier(jnp.sum(velocity * velocity, axis=0)))
    return (density, velocity, pressure)

def speed_fix(value, sound):
    magnitude = jnp.abs(value)
    delta = 0.1 * sound
    return jnp.where(magnitude < delta, (value * value + delta * delta) / (2.0 * delta), magnitude)

def roe_flux(left, right, axis, grid_speed):
    normal = unit_vector(axis, left.ndim - 1)
    rho_l, vel_l, p_l = primitives(left)
    rho_r, vel_r, p_r = primitives(right)
    enth_l = (left[4] + p_l) / rho_l
    enth_r = (right[4] + p_r) / rho_r
    flux_l = (vel_l[axis] - grid_speed) * left + jnp.concatenate([jnp.zeros_like(p_l)[None], p_l[None] * normal, (p_l * vel_l[axis])[None]], 0)
    flux_r = (vel_r[axis] - grid_speed) * right + jnp.concatenate([jnp.zeros_like(p_r)[None], p_r[None] * normal, (p_r * vel_r[axis])[None]], 0)
    ratio = jnp.sqrt(rho_r / rho_l)
    weight_l = 1.0 / (1.0 + ratio)
    weight_r = ratio / (1.0 + ratio)
    vel_t = weight_l * vel_l + weight_r * vel_r
    enth_t = weight_l * enth_l + weight_r * enth_r
    speed_sq = lax.optimization_barrier(jnp.sum(vel_t * vel_t, axis=0))
    sound_sq = (GAMMA - 1.0) * (enth_t - 0.5 * speed_sq)
    sound = jnp.sqrt(sound_sq)
    rho_t = jnp.sqrt(rho_l * rho_r)
    normal_t = vel_t[axis]
    jump_p = p_r - p_l
    jump_rho = rho_r - rho_l
    jump_vel = vel_r - vel_l
    jump_n = jump_vel[axis]
    alpha_one = (jump_p - rho_t * sound * jump_n) / (2.0 * sound_sq)
    alpha_three = (jump_p + rho_t * sound * jump_n) / (2.0 * sound_sq)
    alpha_two = jump_rho - jump_p / sound_sq
    lam_one = speed_fix(normal_t - grid_speed - sound, sound)
    lam_two = speed_fix(normal_t - grid_speed, sound)
    lam_three = speed_fix(normal_t - grid_speed + sound, sound)
    ones = jnp.ones_like(sound)[None]
    wave_one = jnp.concatenate([ones, vel_t - sound * normal, (enth_t - normal_t * sound)[None]], 0)
    wave_two = jnp.concatenate([ones, vel_t, (0.5 * speed_sq)[None]], 0)
    wave_three = jnp.concatenate([ones, vel_t + sound * normal, (enth_t + normal_t * sound)[None]], 0)
    shear = jnp.concatenate([jnp.zeros_like(sound)[None], jump_vel - jump_n * normal, (lax.optimization_barrier(jnp.sum(vel_t * jump_vel, axis=0)) - normal_t * jump_n)[None]], 0)
    dissip = lam_one * alpha_one * wave_one + lam_two * (alpha_two * wave_two + rho_t * shear) + lam_three * alpha_three * wave_three
    return 0.5 * (flux_l + flux_r) - 0.5 * dissip

def reflect(state, axis):
    return jnp.concatenate([state[:1 + axis], -state[1 + axis:2 + axis], state[2 + axis:]], 0)

def face_pair(left, right, mask_left, mask_right, axis):
    left_state = jnp.where(mask_left > 0, left, reflect(right, axis))
    right_state = jnp.where(mask_right > 0, right, reflect(left, axis))
    return (left_state, right_state)

def divergence(padded, live_mask, link, grid_velocity):
    state = padded[:, 1:-1]
    span_flux = roe_flux(padded[:, :-1], padded[:, 1:], 2, grid_velocity[2])
    total = span_flux[:, 1:] - span_flux[:, :-1]
    ahead = jnp.roll(state, -1, axis=3)
    mask_ahead = jnp.roll(live_mask, -1, axis=2)
    left_i, right_i = face_pair(state, ahead, live_mask, mask_ahead, 0)
    chord_flux = roe_flux(left_i, right_i, 0, grid_velocity[0])
    total = total + chord_flux - jnp.roll(chord_flux, 1, axis=3)
    below = jnp.take(state[:, :, 0, :], link, axis=2)[:, :, None]
    mask_below = jnp.take(live_mask[:, 0, :], link, axis=1)[:, None]
    extended = jnp.concatenate([below, state, state[:, :, -1:]], axis=2)
    mask_ext = jnp.concatenate([mask_below, live_mask, jnp.ones_like(live_mask[:, -1:])], axis=1)
    left_j, right_j = face_pair(extended[:, :, :-1], extended[:, :, 1:], mask_ext[:, :-1], mask_ext[:, 1:], 1)
    normal_flux = roe_flux(left_j, right_j, 1, grid_velocity[1])
    return total + normal_flux[:, :, 1:] - normal_flux[:, :, :-1]

def reference(state, frame_velocity, dtau, live_mask, link):
    flap_matrix = instance_matrix(HF, 0.8)
    gust_matrix = instance_matrix(HG, 1.2944)
    current = state
    for step in range(STEPS):
        flat = current.reshape((HF * HG,) + current.shape[2:])
        speeds = frame_velocity.reshape(HF * HG, 3)

        def one_instance(item):
            field, speed = item
            padded = jnp.concatenate([field[:, :1], field, field[:, -1:]], axis=1)
            return divergence(padded, live_mask, link, speed)
        spatial = lax.map(one_instance, (flat, speeds)).reshape(current.shape)
        flap_term = jnp.einsum('ja,abcxyz->jbcxyz', flap_matrix, current, precision=lax.Precision.HIGHEST)
        gust_term = jnp.einsum('jb,abcxyz->ajcxyz', gust_matrix, current, precision=lax.Precision.HIGHEST)
        residual = spatial + flap_term + gust_term
        current = jnp.where(live_mask > 0, current - dtau * residual, current)
    return current
```

```python
import functools
import math

import jax
import jax.numpy as jnp
import numpy as np
from jax import lax
from jax.experimental import pallas as pl
from jax.experimental.pallas import tpu as pltpu
from jax.sharding import PartitionSpec as P

VISC = 0.12
FLAP_OMEGA = 0.8
GUST_OMEGA = 1.2944

RHO, U, V, W, PR, EN, RT, LIVE = range(8)
PAD = 8


def instance_matrix(count, omega):
    offset = np.arange(count)[:, None] - np.arange(count)[None, :]
    angle = np.pi * offset / count
    parity = np.where(offset % 2 == 0, 1.0, -1.0)
    off = offset != 0
    safe = np.where(off, angle, 0.5 * np.pi)
    first = np.where(off, 0.5 * parity / np.tan(safe), 0.0)
    second = np.where(off, -0.5 * parity / np.sin(safe) ** 2, -(count * count / 12.0 + 1.0 / 6.0))
    return omega * first - VISC * second


def primitives(rho, m1, m2, m3, energy):
    inv = 1.0 / rho
    u, v, w = m1 * inv, m2 * inv, m3 * inv
    p = 0.4 * (energy - 0.5 * (m1 * u + m2 * v + m3 * w))
    return (rho, u, v, w, p, (energy + p) * inv, jnp.sqrt(jnp.abs(rho)))


def physical(cell, axis, g):
    rho, vel, p, enth = cell[RHO], cell[U : W + 1], cell[PR], cell[EN]
    mass = rho * (vel[axis] - g)
    mom = [mass * vel[a] + p if a == axis else mass * vel[a] for a in range(3)]
    return [mass, *mom, mass * enth + g * p]


def roe(left, right, axis, g):
    rho_l, vel_l, p_l, h_l, s_l = left[RHO], left[U : W + 1], left[PR], left[EN], left[RT]
    rho_r, vel_r, p_r, h_r, s_r = right[RHO], right[U : W + 1], right[PR], right[EN], right[RT]
    t1, t2 = [a for a in range(3) if a != axis]
    weight = s_r / (s_l + s_r)
    jump = [vel_r[a] - vel_l[a] for a in range(3)]
    vel = [vel_l[a] + weight * jump[a] for a in range(3)]
    enth = h_l + weight * (h_r - h_l)
    half_sq = 0.5 * (vel[0] * vel[0] + vel[1] * vel[1] + vel[2] * vel[2])
    c_sq = 0.4 * (enth - half_sq)
    inv_c = lax.rsqrt(c_sq)
    c = c_sq * inv_c
    delta = 0.1 * c
    scale = 5.0 * inv_c
    half_inv_sq = 0.5 * (inv_c * inv_c)
    rho_t = s_l * s_r
    dp = p_r - p_l
    drho = rho_r - rho_l
    swing = rho_t * c * jump[axis]

    def speed(value):
        size = jnp.abs(value)
        return jnp.where(size < delta, (value * value + delta * delta) * scale, size)

    rel = vel[axis] - g
    l2 = speed(rel)
    w1 = speed(rel - c) * ((dp - swing) * half_inv_sq)
    w3 = speed(rel + c) * ((dp + swing) * half_inv_sq)
    w2 = l2 * (drho - dp * (2.0 * half_inv_sq))
    shear = l2 * rho_t
    acoustic = w1 + w3
    total = acoustic + w2
    skew = (w3 - w1) * c
    mass_l = rho_l * (vel_l[axis] - g)
    mass_r = rho_r * (vel_r[axis] - g)
    out = [0.5 * (mass_l + mass_r - total)]
    for a in range(3):
        flux = mass_l * vel_l[a] + mass_r * vel_r[a]
        if a == axis:
            flux = flux + (p_l + p_r) - (total * vel[a] + skew)
        else:
            flux = flux - (total * vel[a] + shear * jump[a])
        out.append(0.5 * flux)
    loss = acoustic * enth + w2 * half_sq + skew * vel[axis]
    loss = loss + shear * (vel[t1] * jump[t1] + vel[t2] * jump[t2])
    out.append(0.5 * (mass_l * h_l + mass_r * h_r + g * (p_l + p_r) - loss))
    return out


def walled(left, right, axis):
    live_l, live_r = left[LIVE] > 0.0, right[LIVE] > 0.0
    n = U + axis
    new_l, new_r = [], []
    for f in range(LIVE):
        if f == n:
            new_l.append(jnp.where(live_l, left[f], -right[f]))
            new_r.append(jnp.where(live_r, right[f], -left[f]))
        else:
            new_l.append(jnp.where(live_l, left[f], right[f]))
            new_r.append(jnp.where(live_r, right[f], left[f]))
    return new_l, new_r


def divergence_blocks(load, halo_ref, mask_ref, link_ref, speed_ref, first, cells, faces, emit):
    nj = mask_ref.shape[1]
    blocks = nj // 8
    g0, g1, g2 = speed_ref[0], speed_ref[1], speed_ref[2]
    first = first > 0

    def rows(b):
        return pl.multiple_of(8 * b, 8)

    def fill(b, carry):
        row = rows(b)
        for k in range(2):
            values = primitives(*[load(f, k, row) for f in range(5)])
            for f, value in enumerate(values):
                cells[f, k, pl.ds(PAD + row, 8), :] = value
            live = jnp.where(mask_ref[k, pl.ds(row, 8), :] > 0, 1.0, 0.0)
            cells[LIVE, k, pl.ds(PAD + row, 8), :] = live
        return carry

    lax.fori_loop(0, blocks, fill, 0)
    link = jnp.broadcast_to(link_ref[...], (8, link_ref.shape[1]))
    for k in range(2):
        for f in range(8):
            top = cells[f, k, pl.ds(PAD, 8), :]
            cells[f, k, pl.ds(0, 8), :] = jnp.take_along_axis(top, link, axis=1)
            below = cells[f, k, pl.ds(0, 1), :]
            cells[f, k, pl.ds(PAD - 1, 1), :] = below
            last = cells[f, k, pl.ds(PAD + nj - 1, 1), :]
            if f == LIVE:
                last = jnp.ones_like(last)
            cells[f, k, pl.ds(PAD + nj, 8), :] = jnp.broadcast_to(last, (8, last.shape[1]))

    def normal(b, carry):
        row = rows(b)
        for k in range(2):
            left = [cells[f, k, pl.ds(PAD - 1 + row, 8), :] for f in range(8)]
            right = [cells[f, k, pl.ds(PAD + row, 8), :] for f in range(8)]
            flux = roe(*walled(left, right, 1), 1, g1)
            for f in range(5):
                faces[f, k, pl.ds(row, 8), :] = flux[f]
        return carry

    lax.fori_loop(0, blocks + 1, normal, 0)

    def rest(b, carry):
        row = rows(b)
        near = [[cells[f, k, pl.ds(PAD + row, 8), :] for f in range(8)] for k in range(2)]
        halo = primitives(*[halo_ref[f, pl.ds(row, 8), :] for f in range(5)])
        inner = roe(near[0], near[1], 2, g2)
        edge = physical([jnp.where(first, near[0][f], near[1][f]) for f in range(7)], 2, g2)
        left = [jnp.where(first, near[1][f], halo[f]) for f in range(7)]
        right = [jnp.where(first, halo[f], near[0][f]) for f in range(7)]
        outer = roe(left, right, 2, g2)
        for k in range(2):
            here = near[k]
            lanes = here[0].shape[1]
            ahead = [pltpu.roll(x, lanes - 1, 1) for x in here]
            chord = roe(*walled(here, ahead, 0), 0, g0)
            for f in range(5):
                after = faces[f, k, pl.ds(row + 1, 8), :] - faces[f, k, pl.ds(row, 8), :]
                after = after + (chord[f] - pltpu.roll(chord[f], 1, 1))
                if k == 0:
                    span = inner[f] - jnp.where(first, edge[f], outer[f])
                else:
                    span = jnp.where(first, outer[f], edge[f]) - inner[f]
                emit(f, k, row, span + after)
        return carry

    lax.fori_loop(0, blocks, rest, 0)


def scratch(nj, ni):
    return [
        pltpu.VMEM((8, 2, nj + 2 * PAD, ni), jnp.float32),
        pltpu.VMEM((5, 2, nj + PAD, ni), jnp.float32),
    ]


def packed(f, row, q, nj):
    return pl.ds(4 * (f * nj + row) + q, 8, stride=4)


def first_kernel(place_ref, speed_ref, state_ref, halo_ref, mask_ref, link_ref, out_ref, cells, faces):
    nj = mask_ref.shape[1]

    def load(f, k, row):
        return state_ref[f, k, pl.ds(row, 8), :]

    def emit(f, k, row, div):
        out_ref[packed(f, row, k, nj), :] = load(f, k, row)
        out_ref[packed(f, row, 2 + k, nj), :] = div

    used = 4 * 5 * nj
    if out_ref.shape[0] > used:
        out_ref[used:, :] = jnp.zeros((out_ref.shape[0] - used, out_ref.shape[1]), jnp.float32)
    divergence_blocks(load, halo_ref, mask_ref, link_ref, speed_ref, place_ref[0], cells, faces, emit)


def last_kernel(place_ref, speed_ref, turned_ref, halo_ref, mask_ref, dtau_ref, link_ref, out_ref, cells, faces):
    nj = mask_ref.shape[1]

    def load(f, k, row):
        return turned_ref[packed(f, row, k, nj), :]

    def emit(f, k, row, div):
        old = load(f, k, row)
        residual = div + turned_ref[packed(f, row, 2 + k, nj), :]
        live = mask_ref[k, pl.ds(row, 8), :] > 0
        new = old - dtau_ref[k, pl.ds(row, 8), :] * residual
        out_ref[f, k, pl.ds(row, 8), :] = jnp.where(live, new, old)

    divergence_blocks(load, halo_ref, mask_ref, link_ref, speed_ref, place_ref[0], cells, faces, emit)


def edge_kernel(place_ref, turned_ref, out_ref):
    nj = out_ref.shape[1]
    for f in range(5):
        for row in range(0, nj, 8):
            out_ref[f, pl.ds(row, 8), :] = turned_ref[packed(f, row, place_ref[0], nj), :]


def instances_kernel(chunk_ref, matrix_ref, turned_ref, dtau_ref, mask_ref, out_ref):
    count = matrix_ref.shape[0]
    nj = mask_ref.shape[1]
    j = lax.rem(chunk_ref[0], nj)
    parts = [turned_ref[pl.ds(q, count, stride=4), :] for q in range(4)]
    state = jnp.concatenate(parts[:2], axis=1)
    div = jnp.concatenate(parts[2:], axis=1)
    dtau = jnp.concatenate([dtau_ref[k, pl.ds(j, 1), :] for k in range(2)], axis=1)
    mask = jnp.concatenate([mask_ref[k, pl.ds(j, 1), :] for k in range(2)], axis=1)
    matrix = matrix_ref[...]

    def times(x):
        return jnp.dot(matrix, x, precision=lax.Precision.HIGHEST, preferred_element_type=jnp.float32)

    new = state - dtau * (div + times(state))
    new = jnp.where(mask > 0, new, state)
    coupled = times(new)
    lanes = dtau_ref.shape[2]
    for q, value in enumerate((new[:, :lanes], new[:, lanes:], coupled[:, :lanes], coupled[:, lanes:])):
        out_ref[pl.ds(q, count, stride=4), :] = value


def call(kernel, shape, args, smem, scratch_shapes=(), flops=0):
    vmem = pl.BlockSpec(memory_space=pltpu.VMEM)
    specs = [pl.BlockSpec(memory_space=pltpu.SMEM)] * smem + [vmem] * (len(args) - smem)
    args = list(args[:smem]) + [pltpu.with_memory_space_constraint(a, pltpu.VMEM) for a in args[smem:]]
    return pl.pallas_call(
        kernel,
        out_shape=pltpu.VMEM(shape, jnp.float32),
        in_specs=specs,
        out_specs=vmem,
        scratch_shapes=list(scratch_shapes),
        cost_estimate=pl.CostEstimate(flops=flops, bytes_accessed=4 * math.prod(shape), transcendentals=0),
        compiler_params=pltpu.CompilerParams(vmem_limit_bytes=24 * 2**20),
    )(*args)


def shards(matrix, state, frame_velocity, dtau, live_mask, link):
    nj, ni = live_mask.shape[1:]
    flaps, gusts = lax.axis_size("flap"), lax.axis_size("gust")
    count = flaps * gusts
    field = state[0, 0]
    speed = frame_velocity[0, 0]
    link = link[None]
    span = lax.axis_index("span")
    first = jnp.where(span == 0, 1, 0).astype(jnp.int32)[None]
    chunk = (lax.axis_index("flap") * gusts + lax.axis_index("gust")).astype(jnp.int32)[None]
    swap = [(0, 1), (1, 0)]

    def turn(x):
        y = lax.all_to_all(x.reshape(count, 4, ni), ("flap", "gust"), 0, 0, tiled=True)
        return y.reshape(count * 4, ni)

    with jax.named_scope("halo"):
        halo = lax.ppermute(jnp.where(span == 0, field[:, 1], field[:, 0]), "span", swap)
    with jax.named_scope("first_divergence"):
        pack = call(
            first_kernel, (count * 4, ni), (first, speed, field, halo, live_mask, link), 2, scratch(nj, ni), 10**7
        )
    with jax.named_scope("turn"):
        pack = turn(pack)
    with jax.named_scope("instances"):
        pack = call(instances_kernel, (count * 4, ni), (chunk, matrix, pack, dtau, live_mask), 1, (), 10**8)
    with jax.named_scope("turn_back"):
        pack = turn(pack)
    with jax.named_scope("halo"):
        edge = call(edge_kernel, (5, nj, ni), (first, pack), 1)
        halo = lax.ppermute(edge, "span", swap)
    with jax.named_scope("last_divergence"):
        out = call(
            last_kernel,
            field.shape,
            (first, speed, pack, halo, live_mask, dtau, link),
            2,
            scratch(nj, ni),
            10**7,
        )
    return out[None, None]


def solution(mesh):
    flap = instance_matrix(mesh.shape["flap"], FLAP_OMEGA)
    gust = instance_matrix(mesh.shape["gust"], GUST_OMEGA)
    matrix = np.kron(flap, np.eye(len(gust))) + np.kron(np.eye(len(flap)), gust)
    matrix = jnp.asarray(matrix.astype(np.float32))
    in_specs = (
        P("flap", "gust", None, "span", None, None),
        P("flap", "gust", None),
        P("span", None, None),
        P("span", None, None),
        P(),
    )
    out_specs = P("flap", "gust", None, "span", None, None)
    return jax.shard_map(
        functools.partial(shards, matrix), mesh=mesh, in_specs=in_specs, out_specs=out_specs, check_vma=False
    )
```

```python
import functools
import math

import jax
import jax.numpy as jnp
import numpy as np
from jax import lax
from jax.experimental import pallas as pl
from jax.experimental.pallas import tpu as pltpu
from jax.sharding import PartitionSpec as P

VISC = 0.12
FLAP_OMEGA = 0.8
GUST_OMEGA = 1.2944

RHO, U, V, W, PR, EN, RT, LIVE = range(8)
PAD = 8


def instance_matrix(count, omega):
    offset = np.arange(count)[:, None] - np.arange(count)[None, :]
    angle = np.pi * offset / count
    parity = np.where(offset % 2 == 0, 1.0, -1.0)
    off = offset != 0
    safe = np.where(off, angle, 0.5 * np.pi)
    first = np.where(off, 0.5 * parity / np.tan(safe), 0.0)
    second = np.where(off, -0.5 * parity / np.sin(safe) ** 2, -(count * count / 12.0 + 1.0 / 6.0))
    return omega * first - VISC * second


def primitives(rho, m1, m2, m3, energy):
    inv = 1.0 / rho
    u, v, w = m1 * inv, m2 * inv, m3 * inv
    p = 0.4 * (energy - 0.5 * (m1 * u + m2 * v + m3 * w))
    return (rho, u, v, w, p, (energy + p) * inv, jnp.sqrt(jnp.abs(rho)))


def physical(cell, axis, g):
    rho, vel, p, enth = cell[RHO], cell[U : W + 1], cell[PR], cell[EN]
    mass = rho * (vel[axis] - g)
    mom = [mass * vel[a] + p if a == axis else mass * vel[a] for a in range(3)]
    return [mass, *mom, mass * enth + g * p]


def roe(left, right, axis, g):
    rho_l, vel_l, p_l, h_l, s_l = left[RHO], left[U : W + 1], left[PR], left[EN], left[RT]
    rho_r, vel_r, p_r, h_r, s_r = right[RHO], right[U : W + 1], right[PR], right[EN], right[RT]
    t1, t2 = [a for a in range(3) if a != axis]
    weight = s_r / (s_l + s_r)
    jump = [vel_r[a] - vel_l[a] for a in range(3)]
    vel = [vel_l[a] + weight * jump[a] for a in range(3)]
    enth = h_l + weight * (h_r - h_l)
    half_sq = 0.5 * (vel[0] * vel[0] + vel[1] * vel[1] + vel[2] * vel[2])
    c_sq = 0.4 * (enth - half_sq)
    inv_c = lax.rsqrt(c_sq)
    c = c_sq * inv_c
    delta = 0.1 * c
    scale = 5.0 * inv_c
    half_inv_sq = 0.5 * (inv_c * inv_c)
    rho_t = s_l * s_r
    dp = p_r - p_l
    drho = rho_r - rho_l
    swing = rho_t * c * jump[axis]

    def speed(value):
        size = jnp.abs(value)
        return jnp.where(size < delta, (value * value + delta * delta) * scale, size)

    rel = vel[axis] - g
    l2 = speed(rel)
    w1 = speed(rel - c) * ((dp - swing) * half_inv_sq)
    w3 = speed(rel + c) * ((dp + swing) * half_inv_sq)
    w2 = l2 * (drho - dp * (2.0 * half_inv_sq))
    shear = l2 * rho_t
    acoustic = w1 + w3
    total = acoustic + w2
    skew = (w3 - w1) * c
    mass_l = rho_l * (vel_l[axis] - g)
    mass_r = rho_r * (vel_r[axis] - g)
    out = [0.5 * (mass_l + mass_r - total)]
    for a in range(3):
        flux = mass_l * vel_l[a] + mass_r * vel_r[a]
        if a == axis:
            flux = flux + (p_l + p_r) - (total * vel[a] + skew)
        else:
            flux = flux - (total * vel[a] + shear * jump[a])
        out.append(0.5 * flux)
    loss = acoustic * enth + w2 * half_sq + skew * vel[axis]
    loss = loss + shear * (vel[t1] * jump[t1] + vel[t2] * jump[t2])
    out.append(0.5 * (mass_l * h_l + mass_r * h_r + g * (p_l + p_r) - loss))
    return out


def walled(left, right, axis):
    live_l, live_r = left[LIVE] > 0.0, right[LIVE] > 0.0
    n = U + axis
    new_l, new_r = [], []
    for f in range(LIVE):
        if f == n:
            new_l.append(jnp.where(live_l, left[f], -right[f]))
            new_r.append(jnp.where(live_r, right[f], -left[f]))
        else:
            new_l.append(jnp.where(live_l, left[f], right[f]))
            new_r.append(jnp.where(live_r, right[f], left[f]))
    return new_l, new_r


def most_of_divergence(load, mask_ref, link_ref, speed_ref, first, cells, faces, emit):
    nj = mask_ref.shape[1]
    blocks = nj // 8
    g0, g1, g2 = speed_ref[0], speed_ref[1], speed_ref[2]

    def rows(b):
        return pl.multiple_of(8 * b, 8)

    def fill(b, carry):
        row = rows(b)
        for k in range(2):
            values = primitives(*[load(f, k, row) for f in range(5)])
            for f, value in enumerate(values):
                cells[f, k, pl.ds(PAD + row, 8), :] = value
            live = jnp.where(mask_ref[k, pl.ds(row, 8), :] > 0, 1.0, 0.0)
            cells[LIVE, k, pl.ds(PAD + row, 8), :] = live
        return carry

    lax.fori_loop(0, blocks, fill, 0)
    link = jnp.broadcast_to(link_ref[...], (8, link_ref.shape[1]))
    for k in range(2):
        for f in range(8):
            top = cells[f, k, pl.ds(PAD, 8), :]
            below = jnp.take_along_axis(top, link, axis=1)[:1]
            cells[f, k, pl.ds(PAD - 1, 1), :] = below
            last = cells[f, k, pl.ds(PAD + nj - 1, 1), :]
            if f == LIVE:
                last = jnp.ones_like(last)
            cells[f, k, pl.ds(PAD + nj, 8), :] = jnp.broadcast_to(last, (8, last.shape[1]))

    def normal(b, carry):
        row = rows(b)
        for k in range(2):
            left = [cells[f, k, pl.ds(PAD - 1 + row, 8), :] for f in range(8)]
            right = [cells[f, k, pl.ds(PAD + row, 8), :] for f in range(8)]
            flux = roe(*walled(left, right, 1), 1, g1)
            for f in range(5):
                faces[f, k, pl.ds(row, 8), :] = flux[f]
        return carry

    lax.fori_loop(0, blocks + 1, normal, 0)

    def rest(b, carry):
        row = rows(b)
        near = [[cells[f, k, pl.ds(PAD + row, 8), :] for f in range(8)] for k in range(2)]
        inner = roe(near[0], near[1], 2, g2)
        edge = physical([jnp.where(first, near[0][f], near[1][f]) for f in range(7)], 2, g2)
        for k in range(2):
            here = near[k]
            lanes = here[0].shape[1]
            ahead = [pltpu.roll(x, lanes - 1, 1) for x in here]
            chord = roe(*walled(here, ahead, 0), 0, g0)
            for f in range(5):
                after = faces[f, k, pl.ds(row + 1, 8), :] - faces[f, k, pl.ds(row, 8), :]
                after = after + (chord[f] - pltpu.roll(chord[f], 1, 1))
                if k == 0:
                    span = inner[f] - jnp.where(first, edge[f], 0.0)
                else:
                    span = jnp.where(first, 0.0, edge[f]) - inner[f]
                emit(f, k, row, span + after)
        return carry

    lax.fori_loop(0, blocks, rest, 0)


def outer_face(mine, other, speed_ref, first):
    mine, other = primitives(*mine), primitives(*other)
    left = [jnp.where(first, a, b) for a, b in zip(mine, other)]
    right = [jnp.where(first, b, a) for a, b in zip(mine, other)]
    sign = jnp.where(first, 1.0, -1.0)
    return [sign * x for x in roe(left, right, 2, speed_ref[2])]


def scratch(nj, ni):
    return [
        pltpu.VMEM((8, 2, nj + 2 * PAD, ni), jnp.float32),
        pltpu.VMEM((5, 2, nj + PAD, ni), jnp.float32),
    ]


def packed(f, row, q, nj):
    return pl.ds(4 * (f * nj + row) + q, 8, stride=4)


def first_kernel(place_ref, speed_ref, state_ref, mask_ref, link_ref, out_ref, cells, faces):
    def load(f, k, row):
        return state_ref[f, k, pl.ds(row, 8), :]

    def emit(f, k, row, div):
        out_ref[f, k, pl.ds(row, 8), :] = div

    most_of_divergence(load, mask_ref, link_ref, speed_ref, place_ref[0] > 0, cells, faces, emit)


def first_edge_kernel(place_ref, speed_ref, state_ref, other_ref, div_ref, out_ref):
    nj = state_ref.shape[2]
    edge = place_ref[0]
    first = edge > 0
    used = 4 * 5 * nj
    if out_ref.shape[0] > used:
        out_ref[used:, :] = jnp.zeros((out_ref.shape[0] - used, out_ref.shape[1]), jnp.float32)
    for row in range(0, nj, 8):
        block = pl.ds(row, 8)
        mine = [state_ref[f, edge, block, :] for f in range(5)]
        other = [other_ref[f, 1 - edge, block, :] for f in range(5)]
        flux = outer_face(mine, other, speed_ref, first)
        for f in range(5):
            out_ref[packed(f, row, edge, nj), :] = mine[f]
            out_ref[packed(f, row, 1 - edge, nj), :] = state_ref[f, 1 - edge, block, :]
            out_ref[packed(f, row, 2 + edge, nj), :] = div_ref[f, edge, block, :] + flux[f]
            out_ref[packed(f, row, 3 - edge, nj), :] = div_ref[f, 1 - edge, block, :]


def last_kernel(place_ref, speed_ref, turned_ref, mask_ref, link_ref, out_ref, cells, faces):
    nj = mask_ref.shape[1]

    def load(f, k, row):
        return turned_ref[packed(f, row, k, nj), :]

    def emit(f, k, row, div):
        out_ref[f, k, pl.ds(row, 8), :] = div + turned_ref[packed(f, row, 2 + k, nj), :]

    most_of_divergence(load, mask_ref, link_ref, speed_ref, place_ref[0] > 0, cells, faces, emit)


def last_edge_kernel(place_ref, speed_ref, turned_ref, other_ref, residual_ref, mask_ref, dtau_ref, out_ref):
    nj = mask_ref.shape[1]
    edge = place_ref[0]
    first = edge > 0
    for row in range(0, nj, 8):
        block = pl.ds(row, 8)
        mine = [turned_ref[packed(f, row, edge, nj), :] for f in range(5)]
        flux = outer_face(mine, [other_ref[f, block, :] for f in range(5)], speed_ref, first)
        for k in (edge, 1 - edge):
            live = mask_ref[k, block, :] > 0
            dtau = dtau_ref[k, block, :]
            for f in range(5):
                residual = residual_ref[f, k, block, :]
                if k is edge:
                    old, residual = mine[f], residual + flux[f]
                else:
                    old = turned_ref[packed(f, row, k, nj), :]
                out_ref[f, k, block, :] = jnp.where(live, old - dtau * residual, old)


def edge_kernel(place_ref, turned_ref, out_ref):
    nj = out_ref.shape[1]
    for f in range(5):
        for row in range(0, nj, 8):
            out_ref[f, pl.ds(row, 8), :] = turned_ref[packed(f, row, place_ref[0], nj), :]


def instances_kernel(chunk_ref, matrix_ref, turned_ref, dtau_ref, mask_ref, out_ref):
    count = matrix_ref.shape[0]
    nj = mask_ref.shape[1]
    j = lax.rem(chunk_ref[0], nj)
    parts = [turned_ref[pl.ds(q, count, stride=4), :] for q in range(4)]
    state = jnp.concatenate(parts[:2], axis=1)
    div = jnp.concatenate(parts[2:], axis=1)
    dtau = jnp.concatenate([dtau_ref[k, pl.ds(j, 1), :] for k in range(2)], axis=1)
    mask = jnp.concatenate([mask_ref[k, pl.ds(j, 1), :] for k in range(2)], axis=1)
    matrix = matrix_ref[...]

    def times(x):
        return jnp.dot(matrix, x, precision=lax.Precision.HIGHEST, preferred_element_type=jnp.float32)

    new = state - dtau * (div + times(state))
    new = jnp.where(mask > 0, new, state)
    coupled = times(new)
    lanes = dtau_ref.shape[2]
    for q, value in enumerate((new[:, :lanes], new[:, lanes:], coupled[:, :lanes], coupled[:, lanes:])):
        out_ref[pl.ds(q, count, stride=4), :] = value


def call(kernel, shape, args, smem, scratch_shapes=(), flops=0, keep=True):
    vmem = pl.BlockSpec(memory_space=pltpu.VMEM)
    specs = [pl.BlockSpec(memory_space=pltpu.SMEM)] * smem + [vmem] * (len(args) - smem)
    args = list(args[:smem]) + [pltpu.with_memory_space_constraint(a, pltpu.VMEM) for a in args[smem:]]
    return pl.pallas_call(
        kernel,
        out_shape=pltpu.VMEM(shape, jnp.float32) if keep else jax.ShapeDtypeStruct(shape, jnp.float32),
        in_specs=specs,
        out_specs=vmem,
        scratch_shapes=list(scratch_shapes),
        cost_estimate=pl.CostEstimate(flops=flops, bytes_accessed=4 * math.prod(shape), transcendentals=0),
        compiler_params=pltpu.CompilerParams(vmem_limit_bytes=24 * 2**20),
    )(*args)


def shards(matrix, state, frame_velocity, dtau, live_mask, link):
    nj, ni = live_mask.shape[1:]
    flaps, gusts = lax.axis_size("flap"), lax.axis_size("gust")
    count = flaps * gusts
    field = state[0, 0]
    speed = frame_velocity[0, 0]
    link = link[None]
    first = jnp.where(lax.axis_index("span") == 0, 1, 0).astype(jnp.int32)[None]
    chunk = (lax.axis_index("flap") * gusts + lax.axis_index("gust")).astype(jnp.int32)[None]
    swap = [(0, 1), (1, 0)]

    def turn(x):
        y = lax.all_to_all(x.reshape(count, 4, ni), ("flap", "gust"), 0, 0, tiled=True)
        return y.reshape(count * 4, ni)

    with jax.named_scope("halo"):
        other = lax.ppermute(field, "span", swap)
    with jax.named_scope("first_divergence"):
        div = call(first_kernel, field.shape, (first, speed, field, live_mask, link), 2, scratch(nj, ni), 10**8)
        pack = call(first_edge_kernel, (count * 4, ni), (first, speed, field, other, div), 2)
    with jax.named_scope("turn"):
        pack = turn(pack)
    with jax.named_scope("instances"):
        pack = call(instances_kernel, (count * 4, ni), (chunk, matrix, pack, dtau, live_mask), 1, (), 10**8)
    with jax.named_scope("turn_back"):
        pack = turn(pack)
    with jax.named_scope("halo"):
        other = lax.ppermute(call(edge_kernel, (5, nj, ni), (first, pack), 1), "span", swap)
    with jax.named_scope("last_divergence"):
        residual = call(last_kernel, field.shape, (first, speed, pack, live_mask, link), 2, scratch(nj, ni), 10**8)
        out = call(
            last_edge_kernel, field.shape, (first, speed, pack, other, residual, live_mask, dtau), 2, keep=False
        )
    return out[None, None]


def solution(mesh):
    flap = instance_matrix(mesh.shape["flap"], FLAP_OMEGA)
    gust = instance_matrix(mesh.shape["gust"], GUST_OMEGA)
    matrix = np.kron(flap, np.eye(len(gust))) + np.kron(np.eye(len(flap)), gust)
    matrix = jnp.asarray(matrix.astype(np.float32))
    in_specs = (
        P("flap", "gust", None, "span", None, None),
        P("flap", "gust", None),
        P("span", None, None),
        P("span", None, None),
        P(),
    )
    out_specs = P("flap", "gust", None, "span", None, None)
    return jax.shard_map(
        functools.partial(shards, matrix), mesh=mesh, in_specs=in_specs, out_specs=out_specs, check_vma=False
    )
```

```python
import functools
import math

import jax
import jax.numpy as jnp
import numpy as np
from jax import lax
from jax.experimental import pallas as pl
from jax.experimental.pallas import tpu as pltpu
from jax.sharding import PartitionSpec as P

VISC = 0.12
FLAP_OMEGA = 0.8
GUST_OMEGA = 1.2944

RHO, U, V, W, PR, EN, RT, LIVE = range(8)
PAD = 8


def instance_matrix(count, omega):
    offset = np.arange(count)[:, None] - np.arange(count)[None, :]
    angle = np.pi * offset / count
    parity = np.where(offset % 2 == 0, 1.0, -1.0)
    off = offset != 0
    safe = np.where(off, angle, 0.5 * np.pi)
    first = np.where(off, 0.5 * parity / np.tan(safe), 0.0)
    second = np.where(off, -0.5 * parity / np.sin(safe) ** 2, -(count * count / 12.0 + 1.0 / 6.0))
    return omega * first - VISC * second


def primitives(rho, m1, m2, m3, energy):
    inv = 1.0 / rho
    u, v, w = m1 * inv, m2 * inv, m3 * inv
    p = 0.4 * (energy - 0.5 * (m1 * u + m2 * v + m3 * w))
    return (rho, u, v, w, p, (energy + p) * inv, jnp.sqrt(jnp.abs(rho)))


def physical(cell, axis, g):
    rho, vel, p, enth = cell[RHO], cell[U : W + 1], cell[PR], cell[EN]
    mass = rho * (vel[axis] - g)
    mom = [mass * vel[a] + p if a == axis else mass * vel[a] for a in range(3)]
    return [mass, *mom, mass * enth + g * p]


def roe(left, right, axis, g):
    rho_l, vel_l, p_l, h_l, s_l = left[RHO], left[U : W + 1], left[PR], left[EN], left[RT]
    rho_r, vel_r, p_r, h_r, s_r = right[RHO], right[U : W + 1], right[PR], right[EN], right[RT]
    t1, t2 = [a for a in range(3) if a != axis]
    weight = s_r / (s_l + s_r)
    jump = [vel_r[a] - vel_l[a] for a in range(3)]
    vel = [vel_l[a] + weight * jump[a] for a in range(3)]
    enth = h_l + weight * (h_r - h_l)
    half_sq = 0.5 * (vel[0] * vel[0] + vel[1] * vel[1] + vel[2] * vel[2])
    c_sq = 0.4 * (enth - half_sq)
    inv_c = lax.rsqrt(c_sq)
    c = c_sq * inv_c
    delta = 0.1 * c
    scale = 5.0 * inv_c
    half_inv_sq = 0.5 * (inv_c * inv_c)
    rho_t = s_l * s_r
    dp = p_r - p_l
    drho = rho_r - rho_l
    swing = rho_t * c * jump[axis]

    def speed(value):
        size = jnp.abs(value)
        return jnp.where(size < delta, (value * value + delta * delta) * scale, size)

    rel = vel[axis] - g
    l2 = speed(rel)
    w1 = speed(rel - c) * ((dp - swing) * half_inv_sq)
    w3 = speed(rel + c) * ((dp + swing) * half_inv_sq)
    w2 = l2 * (drho - dp * (2.0 * half_inv_sq))
    shear = l2 * rho_t
    acoustic = w1 + w3
    total = acoustic + w2
    skew = (w3 - w1) * c
    mass_l = rho_l * (vel_l[axis] - g)
    mass_r = rho_r * (vel_r[axis] - g)
    out = [0.5 * (mass_l + mass_r - total)]
    for a in range(3):
        flux = mass_l * vel_l[a] + mass_r * vel_r[a]
        if a == axis:
            flux = flux + (p_l + p_r) - (total * vel[a] + skew)
        else:
            flux = flux - (total * vel[a] + shear * jump[a])
        out.append(0.5 * flux)
    loss = acoustic * enth + w2 * half_sq + skew * vel[axis]
    loss = loss + shear * (vel[t1] * jump[t1] + vel[t2] * jump[t2])
    out.append(0.5 * (mass_l * h_l + mass_r * h_r + g * (p_l + p_r) - loss))
    return out


def walled(left, right, axis):
    live_l, live_r = left[LIVE] > 0.0, right[LIVE] > 0.0
    n = U + axis
    new_l, new_r = [], []
    for f in range(LIVE):
        if f == n:
            new_l.append(jnp.where(live_l, left[f], -right[f]))
            new_r.append(jnp.where(live_r, right[f], -left[f]))
        else:
            new_l.append(jnp.where(live_l, left[f], right[f]))
            new_r.append(jnp.where(live_r, right[f], left[f]))
    return new_l, new_r


def frame(speed_ref, axis):
    return jnp.broadcast_to(speed_ref[:, axis : axis + 1], (8, 128))


def most_of_divergence(load, mask_ref, link_ref, speed_ref, first, cells, faces, emit):
    nj = mask_ref.shape[1]
    blocks = nj // 8
    g0, g1, g2 = [frame(speed_ref, axis) for axis in range(3)]

    def rows(b):
        return pl.multiple_of(8 * b, 8)

    def fill(b, carry):
        row = rows(b)
        for k in range(2):
            values = primitives(*[load(f, k, row) for f in range(5)])
            for f, value in enumerate(values):
                cells[f, k, pl.ds(PAD + row, 8), :] = value
            live = jnp.where(mask_ref[k, pl.ds(row, 8), :] > 0, 1.0, 0.0)
            cells[LIVE, k, pl.ds(PAD + row, 8), :] = live
        return carry

    lax.fori_loop(0, blocks, fill, 0)
    link = jnp.broadcast_to(link_ref[...], (8, link_ref.shape[1]))
    for k in range(2):
        for f in range(8):
            top = cells[f, k, pl.ds(PAD, 8), :]
            below = jnp.take_along_axis(top, link, axis=1)[:1]
            cells[f, k, pl.ds(PAD - 1, 1), :] = below
            last = cells[f, k, pl.ds(PAD + nj - 1, 1), :]
            if f == LIVE:
                last = jnp.ones_like(last)
            cells[f, k, pl.ds(PAD + nj, 8), :] = jnp.broadcast_to(last, (8, last.shape[1]))

    def normal(b, carry):
        row = rows(b)
        for k in range(2):
            left = [cells[f, k, pl.ds(PAD - 1 + row, 8), :] for f in range(8)]
            right = [cells[f, k, pl.ds(PAD + row, 8), :] for f in range(8)]
            flux = roe(*walled(left, right, 1), 1, g1)
            for f in range(5):
                faces[f, k, pl.ds(row, 8), :] = flux[f]
        return carry

    lax.fori_loop(0, blocks + 1, normal, 0)

    def rest(b, carry):
        row = rows(b)
        near = [[cells[f, k, pl.ds(PAD + row, 8), :] for f in range(8)] for k in range(2)]
        inner = roe(near[0], near[1], 2, g2)
        edge = physical([jnp.where(first, near[0][f], near[1][f]) for f in range(7)], 2, g2)
        for k in range(2):
            here = near[k]
            lanes = here[0].shape[1]
            ahead = [pltpu.roll(x, lanes - 1, 1) for x in here]
            chord = roe(*walled(here, ahead, 0), 0, g0)
            for f in range(5):
                after = faces[f, k, pl.ds(row + 1, 8), :] - faces[f, k, pl.ds(row, 8), :]
                after = after + (chord[f] - pltpu.roll(chord[f], 1, 1))
                if k == 0:
                    span = inner[f] - jnp.where(first, edge[f], 0.0)
                else:
                    span = jnp.where(first, 0.0, edge[f]) - inner[f]
                emit(f, k, row, span + after)
        return carry

    lax.fori_loop(0, blocks, rest, 0)


def outer_face(mine, other, speed_ref, first):
    mine, other = primitives(*mine), primitives(*other)
    left = [jnp.where(first, a, b) for a, b in zip(mine, other)]
    right = [jnp.where(first, b, a) for a, b in zip(mine, other)]
    sign = jnp.where(first, 1.0, -1.0)
    return [sign * x for x in roe(left, right, 2, frame(speed_ref, 2))]


def scratch(nj, ni):
    return [
        pltpu.VMEM((8, 2, nj + 2 * PAD, ni), jnp.float32),
        pltpu.VMEM((5, 2, nj + PAD, ni), jnp.float32),
    ]


def packed(f, row, q, nj):
    return pl.ds(4 * (f * nj + row) + q, 8, stride=4)


def first_kernel(place_ref, *refs):
    sources, targets, (out_ref, cells, faces, state_ref, sems) = refs[:6], refs[6:11], refs[11:]
    mask_ref, link_ref, speed_ref = targets[:3]
    nj = mask_ref.shape[1]
    copies = [
        pltpu.make_async_copy(source, target, sems.at[i])
        for i, (source, target) in enumerate(zip(sources, (state_ref, *targets)))
    ]
    for copy in copies:
        copy.start()
    used = 4 * 5 * nj
    if out_ref.shape[0] > used:
        out_ref[used:, :] = jnp.zeros((out_ref.shape[0] - used, out_ref.shape[1]), jnp.float32)
    for copy in copies[:4]:
        copy.wait()

    def load(f, k, row):
        return state_ref[f, k, pl.ds(row, 8), :]

    def emit(f, k, row, div):
        out_ref[packed(f, row, k, nj), :] = load(f, k, row)
        out_ref[packed(f, row, 2 + k, nj), :] = div

    most_of_divergence(load, mask_ref, link_ref, speed_ref, place_ref[0] > 0, cells, faces, emit)
    for copy in copies[4:]:
        copy.wait()


def first_edge_kernel(place_ref, speed_ref, other_ref, pack_ref, out_ref):
    nj = other_ref.shape[2]
    edge = place_ref[0]
    out_ref[...] = pack_ref[...]
    for row in range(0, nj, 8):
        mine = [pack_ref[packed(f, row, edge, nj), :] for f in range(5)]
        other = [other_ref[f, 1 - edge, pl.ds(row, 8), :] for f in range(5)]
        flux = outer_face(mine, other, speed_ref, edge > 0)
        for f in range(5):
            div = packed(f, row, 2 + edge, nj)
            out_ref[div, :] = pack_ref[div, :] + flux[f]


def last_kernel(place_ref, speed_ref, turned_ref, mask_ref, link_ref, out_ref, cells, faces):
    nj = mask_ref.shape[1]

    def load(f, k, row):
        return turned_ref[packed(f, row, k, nj), :]

    def emit(f, k, row, div):
        out_ref[f, k, pl.ds(row, 8), :] = div + turned_ref[packed(f, row, 2 + k, nj), :]

    most_of_divergence(load, mask_ref, link_ref, speed_ref, place_ref[0] > 0, cells, faces, emit)


def last_edge_kernel(place_ref, speed_ref, turned_ref, other_ref, residual_ref, mask_ref, dtau_ref, out_ref):
    nj = mask_ref.shape[1]
    edge = place_ref[0]
    first = edge > 0
    for row in range(0, nj, 8):
        block = pl.ds(row, 8)
        mine = [turned_ref[packed(f, row, edge, nj), :] for f in range(5)]
        flux = outer_face(mine, [other_ref[f, block, :] for f in range(5)], speed_ref, first)
        for k in (edge, 1 - edge):
            live = mask_ref[k, block, :] > 0
            dtau = dtau_ref[k, block, :]
            for f in range(5):
                residual = residual_ref[f, k, block, :]
                if k is edge:
                    old, residual = mine[f], residual + flux[f]
                else:
                    old = turned_ref[packed(f, row, k, nj), :]
                out_ref[f, k, block, :] = jnp.where(live, old - dtau * residual, old)


def edge_kernel(place_ref, turned_ref, out_ref):
    nj = out_ref.shape[1]
    for f in range(5):
        for row in range(0, nj, 8):
            out_ref[f, pl.ds(row, 8), :] = turned_ref[packed(f, row, place_ref[0], nj), :]


def instances_kernel(place_ref, matrix_ref, turned_ref, dtau_ref, mask_ref, out_ref):
    count = matrix_ref.shape[0]
    nj = mask_ref.shape[1]
    j = lax.rem(place_ref[1], nj)
    parts = [turned_ref[pl.ds(q, count, stride=4), :] for q in range(4)]
    state = jnp.concatenate(parts[:2], axis=1)
    div = jnp.concatenate(parts[2:], axis=1)
    dtau = jnp.concatenate([dtau_ref[k, pl.ds(j, 1), :] for k in range(2)], axis=1)
    mask = jnp.concatenate([mask_ref[k, pl.ds(j, 1), :] for k in range(2)], axis=1)
    matrix = matrix_ref[...]

    def times(x):
        return jnp.dot(matrix, x, precision=lax.Precision.HIGHEST, preferred_element_type=jnp.float32)

    new = state - dtau * (div + times(state))
    new = jnp.where(mask > 0, new, state)
    coupled = times(new)
    lanes = dtau_ref.shape[2]
    for q, value in enumerate((new[:, :lanes], new[:, lanes:], coupled[:, :lanes], coupled[:, lanes:])):
        out_ref[pl.ds(q, count, stride=4), :] = value


def call(kernel, shape, args, scratch_shapes=(), flops=0, aliases=None, keep=True):
    vmem = pl.BlockSpec(memory_space=pltpu.VMEM)
    specs = [pl.BlockSpec(memory_space=pltpu.SMEM)] + [vmem] * (len(args) - 1)
    args = [args[0]] + [pltpu.with_memory_space_constraint(a, pltpu.VMEM) for a in args[1:]]
    return pl.pallas_call(
        kernel,
        out_shape=pltpu.VMEM(shape, jnp.float32) if keep else jax.ShapeDtypeStruct(shape, jnp.float32),
        in_specs=specs,
        out_specs=vmem,
        scratch_shapes=list(scratch_shapes),
        input_output_aliases=aliases or {},
        cost_estimate=pl.CostEstimate(flops=flops, bytes_accessed=4 * math.prod(shape), transcendentals=0),
        compiler_params=pltpu.CompilerParams(vmem_limit_bytes=24 * 2**20),
    )(*args)


def first_call(rows, place, field, mask, link, speed, matrix, dtau):
    vmem = pl.BlockSpec(memory_space=pltpu.VMEM)
    given = (mask, link, speed, matrix, dtau)
    sources = [pltpu.with_memory_space_constraint(a, pltpu.HBM) for a in (field, *given)]
    outs = [pltpu.VMEM(a.shape, a.dtype) for a in given] + [pltpu.VMEM((rows, dtau.shape[2]), jnp.float32)]
    return pl.pallas_call(
        first_kernel,
        out_shape=outs,
        in_specs=[pl.BlockSpec(memory_space=pltpu.SMEM)] + [pl.BlockSpec(memory_space=pltpu.HBM)] * 6,
        out_specs=[vmem] * 6,
        scratch_shapes=[
            *scratch(*mask.shape[1:]),
            pltpu.VMEM(field.shape, jnp.float32),
            pltpu.SemaphoreType.DMA((6,)),
        ],
        cost_estimate=pl.CostEstimate(flops=10**8, bytes_accessed=10**6, transcendentals=0),
        compiler_params=pltpu.CompilerParams(vmem_limit_bytes=24 * 2**20),
    )(place, *sources)


def shards(matrix, state, frame_velocity, dtau, live_mask, link):
    nj, ni = live_mask.shape[1:]
    flaps, gusts = lax.axis_size("flap"), lax.axis_size("gust")
    count = flaps * gusts
    field = state[0, 0]
    first = jnp.where(lax.axis_index("span") == 0, 1, 0)
    place = jnp.stack([first, lax.axis_index("flap") * gusts + lax.axis_index("gust")]).astype(jnp.int32)
    swap = [(0, 1), (1, 0)]

    def turn(x):
        y = lax.all_to_all(x.reshape(count, 4, ni), ("flap", "gust"), 0, 0, tiled=True)
        return y.reshape(count * 4, ni)

    with jax.named_scope("halo"):
        other = lax.ppermute(field, "span", swap)
    with jax.named_scope("first_divergence"):
        mask, link, speed, matrix, dtau, pack = first_call(
            count * 4, place, field, live_mask, link[None], frame_velocity[0], matrix, dtau
        )
        pack = call(first_edge_kernel, pack.shape, (place, speed, other, pack), aliases={3: 0})
    with jax.named_scope("turn"):
        pack = turn(pack)
    with jax.named_scope("instances"):
        pack = call(instances_kernel, pack.shape, (place, matrix, pack, dtau, mask), (), 10**8)
    with jax.named_scope("turn_back"):
        pack = turn(pack)
    with jax.named_scope("halo"):
        other = lax.ppermute(call(edge_kernel, (5, nj, ni), (place, pack)), "span", swap)
    with jax.named_scope("last_divergence"):
        residual = call(last_kernel, field.shape, (place, speed, pack, mask, link), scratch(nj, ni), 10**8)
        out = call(last_edge_kernel, field.shape, (place, speed, pack, other, residual, mask, dtau), keep=False)
    return out[None, None]


def solution(mesh):
    flap = instance_matrix(mesh.shape["flap"], FLAP_OMEGA)
    gust = instance_matrix(mesh.shape["gust"], GUST_OMEGA)
    matrix = np.kron(flap, np.eye(len(gust))) + np.kron(np.eye(len(flap)), gust)
    matrix = jnp.asarray(matrix.astype(np.float32))
    in_specs = (
        P("flap", "gust", None, "span", None, None),
        P("flap", "gust", None),
        P("span", None, None),
        P("span", None, None),
        P(),
    )
    out_specs = P("flap", "gust", None, "span", None, None)
    return jax.shard_map(
        functools.partial(shards, matrix), mesh=mesh, in_specs=in_specs, out_specs=out_specs, check_vma=False
    )
```

```python
import functools
import math

import jax
import jax.numpy as jnp
import numpy as np
from jax import lax
from jax.experimental import pallas as pl
from jax.experimental.pallas import tpu as pltpu
from jax.sharding import PartitionSpec as P

VISC = 0.12
FLAP_OMEGA = 0.8
GUST_OMEGA = 1.2944

RHO, U, V, W, PR, EN, RT, LIVE = range(8)
PAD = 8


def instance_matrix(count, omega):
    offset = np.arange(count)[:, None] - np.arange(count)[None, :]
    angle = np.pi * offset / count
    parity = np.where(offset % 2 == 0, 1.0, -1.0)
    off = offset != 0
    safe = np.where(off, angle, 0.5 * np.pi)
    first = np.where(off, 0.5 * parity / np.tan(safe), 0.0)
    second = np.where(off, -0.5 * parity / np.sin(safe) ** 2, -(count * count / 12.0 + 1.0 / 6.0))
    return omega * first - VISC * second


def primitives(rho, m1, m2, m3, energy):
    inv = 1.0 / rho
    u, v, w = m1 * inv, m2 * inv, m3 * inv
    p = 0.4 * (energy - 0.5 * (m1 * u + m2 * v + m3 * w))
    return (rho, u, v, w, p, (energy + p) * inv, jnp.sqrt(jnp.abs(rho)))


def physical(cell, axis, g):
    rho, vel, p, enth = cell[RHO], cell[U : W + 1], cell[PR], cell[EN]
    mass = rho * (vel[axis] - g)
    mom = [mass * vel[a] + p if a == axis else mass * vel[a] for a in range(3)]
    return [mass, *mom, mass * enth + g * p]


def roe(left, right, axis, g):
    rho_l, vel_l, p_l, h_l, s_l = left[RHO], left[U : W + 1], left[PR], left[EN], left[RT]
    rho_r, vel_r, p_r, h_r, s_r = right[RHO], right[U : W + 1], right[PR], right[EN], right[RT]
    t1, t2 = [a for a in range(3) if a != axis]
    weight = s_r / (s_l + s_r)
    jump = [vel_r[a] - vel_l[a] for a in range(3)]
    vel = [vel_l[a] + weight * jump[a] for a in range(3)]
    enth = h_l + weight * (h_r - h_l)
    half_sq = 0.5 * (vel[0] * vel[0] + vel[1] * vel[1] + vel[2] * vel[2])
    c_sq = 0.4 * (enth - half_sq)
    inv_c = lax.rsqrt(c_sq)
    c = c_sq * inv_c
    delta = 0.1 * c
    scale = 5.0 * inv_c
    half_inv_sq = 0.5 * (inv_c * inv_c)
    rho_t = s_l * s_r
    dp = p_r - p_l
    drho = rho_r - rho_l
    swing = rho_t * c * jump[axis]

    def speed(value):
        size = jnp.abs(value)
        return jnp.where(size < delta, (value * value + delta * delta) * scale, size)

    rel = vel[axis] - g
    l2 = speed(rel)
    w1 = speed(rel - c) * ((dp - swing) * half_inv_sq)
    w3 = speed(rel + c) * ((dp + swing) * half_inv_sq)
    w2 = l2 * (drho - dp * (2.0 * half_inv_sq))
    shear = l2 * rho_t
    acoustic = w1 + w3
    total = acoustic + w2
    skew = (w3 - w1) * c
    mass_l = rho_l * (vel_l[axis] - g)
    mass_r = rho_r * (vel_r[axis] - g)
    out = [0.5 * (mass_l + mass_r - total)]
    for a in range(3):
        flux = mass_l * vel_l[a] + mass_r * vel_r[a]
        if a == axis:
            flux = flux + (p_l + p_r) - (total * vel[a] + skew)
        else:
            flux = flux - (total * vel[a] + shear * jump[a])
        out.append(0.5 * flux)
    loss = acoustic * enth + w2 * half_sq + skew * vel[axis]
    loss = loss + shear * (vel[t1] * jump[t1] + vel[t2] * jump[t2])
    out.append(0.5 * (mass_l * h_l + mass_r * h_r + g * (p_l + p_r) - loss))
    return out


def walled(left, right, axis):
    live_l, live_r = left[LIVE] > 0.0, right[LIVE] > 0.0
    n = U + axis
    new_l, new_r = [], []
    for f in range(LIVE):
        if f == n:
            new_l.append(jnp.where(live_l, left[f], -right[f]))
            new_r.append(jnp.where(live_r, right[f], -left[f]))
        else:
            new_l.append(jnp.where(live_l, left[f], right[f]))
            new_r.append(jnp.where(live_r, right[f], left[f]))
    return new_l, new_r


def frame(speed_ref, axis):
    return jnp.broadcast_to(speed_ref[:, axis : axis + 1], (8, 128))


def most_of_divergence(load, mask_ref, link_ref, speed_ref, first, cells, faces, emit):
    nj = mask_ref.shape[1]
    blocks = nj // 8
    g0, g1, g2 = [frame(speed_ref, axis) for axis in range(3)]

    def rows(b):
        return pl.multiple_of(8 * b, 8)

    def fill(b, carry):
        row = rows(b)
        for k in range(2):
            values = primitives(*[load(f, k, row) for f in range(5)])
            for f, value in enumerate(values):
                cells[f, k, pl.ds(PAD + row, 8), :] = value
            live = jnp.where(mask_ref[k, pl.ds(row, 8), :] > 0, 1.0, 0.0)
            cells[LIVE, k, pl.ds(PAD + row, 8), :] = live
        return carry

    lax.fori_loop(0, blocks, fill, 0, unroll=True)
    link = jnp.broadcast_to(link_ref[...], (8, link_ref.shape[1]))
    for k in range(2):
        for f in range(8):
            top = cells[f, k, pl.ds(PAD, 8), :]
            below = jnp.take_along_axis(top, link, axis=1)[:1]
            cells[f, k, pl.ds(PAD - 1, 1), :] = below
            last = cells[f, k, pl.ds(PAD + nj - 1, 1), :]
            if f == LIVE:
                last = jnp.ones_like(last)
            cells[f, k, pl.ds(PAD + nj, 8), :] = jnp.broadcast_to(last, (8, last.shape[1]))

    def normal(b, carry):
        row = rows(b)
        for k in range(2):
            left = [cells[f, k, pl.ds(PAD - 1 + row, 8), :] for f in range(8)]
            right = [cells[f, k, pl.ds(PAD + row, 8), :] for f in range(8)]
            flux = roe(*walled(left, right, 1), 1, g1)
            for f in range(5):
                faces[f, k, pl.ds(row, 8), :] = flux[f]
        return carry

    lax.fori_loop(0, blocks + 1, normal, 0, unroll=True)

    def rest(b, carry):
        row = rows(b)
        near = [[cells[f, k, pl.ds(PAD + row, 8), :] for f in range(8)] for k in range(2)]
        inner = roe(near[0], near[1], 2, g2)
        edge = physical([jnp.where(first, near[0][f], near[1][f]) for f in range(7)], 2, g2)
        for k in range(2):
            here = near[k]
            lanes = here[0].shape[1]
            ahead = [pltpu.roll(x, lanes - 1, 1) for x in here]
            chord = roe(*walled(here, ahead, 0), 0, g0)
            for f in range(5):
                after = faces[f, k, pl.ds(row + 1, 8), :] - faces[f, k, pl.ds(row, 8), :]
                after = after + (chord[f] - pltpu.roll(chord[f], 1, 1))
                if k == 0:
                    span = inner[f] - jnp.where(first, edge[f], 0.0)
                else:
                    span = jnp.where(first, 0.0, edge[f]) - inner[f]
                emit(f, k, row, span + after)
        return carry

    lax.fori_loop(0, blocks, rest, 0, unroll=True)


def outer_face(mine, other, speed_ref, first):
    mine, other = primitives(*mine), primitives(*other)
    left = [jnp.where(first, a, b) for a, b in zip(mine, other)]
    right = [jnp.where(first, b, a) for a, b in zip(mine, other)]
    sign = jnp.where(first, 1.0, -1.0)
    return [sign * x for x in roe(left, right, 2, frame(speed_ref, 2))]


def scratch(nj, ni):
    return [
        pltpu.VMEM((8, 2, nj + 2 * PAD, ni), jnp.float32),
        pltpu.VMEM((5, 2, nj + PAD, ni), jnp.float32),
    ]


def packed(f, row, q, nj):
    return pl.ds(4 * (f * nj + row) + q, 8, stride=4)


def first_kernel(place_ref, chunk_ref, *refs):
    sources, targets, (out_ref, cells, faces, state_ref, sems) = refs[:6], refs[6:11], refs[11:]
    mask_ref, link_ref, speed_ref = targets[:3]
    nj = mask_ref.shape[1]
    copies = [
        pltpu.make_async_copy(source, target, sems.at[i])
        for i, (source, target) in enumerate(zip(sources, (state_ref, *targets)))
    ]
    for copy in copies:
        copy.start()
    used = 4 * 5 * nj
    if out_ref.shape[0] > used:
        out_ref[used:, :] = jnp.zeros((out_ref.shape[0] - used, out_ref.shape[1]), jnp.float32)
    for copy in copies[:4]:
        copy.wait()

    def load(f, k, row):
        return state_ref[f, k, pl.ds(row, 8), :]

    def emit(f, k, row, div):
        out_ref[packed(f, row, k, nj), :] = load(f, k, row)
        out_ref[packed(f, row, 2 + k, nj), :] = div

    most_of_divergence(load, mask_ref, link_ref, speed_ref, place_ref[0] > 0, cells, faces, emit)
    for copy in copies[4:]:
        copy.wait()


def first_edge_kernel(place_ref, speed_ref, other_ref, pack_ref, out_ref):
    nj = other_ref.shape[2]
    edge = place_ref[0]
    out_ref[...] = pack_ref[...]
    for row in range(0, nj, 8):
        mine = [pack_ref[packed(f, row, edge, nj), :] for f in range(5)]
        other = [other_ref[f, 1 - edge, pl.ds(row, 8), :] for f in range(5)]
        flux = outer_face(mine, other, speed_ref, edge > 0)
        for f in range(5):
            div = packed(f, row, 2 + edge, nj)
            out_ref[div, :] = pack_ref[div, :] + flux[f]


def last_kernel(place_ref, speed_ref, turned_ref, mask_ref, link_ref, out_ref, cells, faces):
    nj = mask_ref.shape[1]

    def load(f, k, row):
        return turned_ref[packed(f, row, k, nj), :]

    def emit(f, k, row, div):
        out_ref[f, k, pl.ds(row, 8), :] = div + turned_ref[packed(f, row, 2 + k, nj), :]

    most_of_divergence(load, mask_ref, link_ref, speed_ref, place_ref[0] > 0, cells, faces, emit)


def last_edge_kernel(place_ref, speed_ref, turned_ref, other_ref, residual_ref, mask_ref, dtau_ref, out_ref):
    nj = mask_ref.shape[1]
    edge = place_ref[0]
    first = edge > 0
    for row in range(0, nj, 8):
        block = pl.ds(row, 8)
        mine = [turned_ref[packed(f, row, edge, nj), :] for f in range(5)]
        flux = outer_face(mine, [other_ref[f, block, :] for f in range(5)], speed_ref, first)
        for k in (edge, 1 - edge):
            live = mask_ref[k, block, :] > 0
            dtau = dtau_ref[k, block, :]
            for f in range(5):
                residual = residual_ref[f, k, block, :]
                if k is edge:
                    old, residual = mine[f], residual + flux[f]
                else:
                    old = turned_ref[packed(f, row, k, nj), :]
                out_ref[f, k, block, :] = jnp.where(live, old - dtau * residual, old)


def edge_kernel(place_ref, turned_ref, out_ref):
    nj = out_ref.shape[1]
    for f in range(5):
        for row in range(0, nj, 8):
            out_ref[f, pl.ds(row, 8), :] = turned_ref[packed(f, row, place_ref[0], nj), :]


def instances_kernel(chunk_ref, matrix_ref, turned_ref, dtau_ref, mask_ref, out_ref):
    count = matrix_ref.shape[0]
    nj = mask_ref.shape[1]
    j = lax.rem(chunk_ref[0], nj)
    parts = [turned_ref[pl.ds(q, count, stride=4), :] for q in range(4)]
    state = jnp.concatenate(parts[:2], axis=1)
    div = jnp.concatenate(parts[2:], axis=1)
    dtau = jnp.concatenate([dtau_ref[k, pl.ds(j, 1), :] for k in range(2)], axis=1)
    mask = jnp.concatenate([mask_ref[k, pl.ds(j, 1), :] for k in range(2)], axis=1)
    matrix = matrix_ref[...]

    def times(x):
        return jnp.dot(matrix, x, precision=lax.Precision.HIGHEST, preferred_element_type=jnp.float32)

    new = state - dtau * (div + times(state))
    new = jnp.where(mask > 0, new, state)
    coupled = times(new)
    lanes = dtau_ref.shape[2]
    for q, value in enumerate((new[:, :lanes], new[:, lanes:], coupled[:, :lanes], coupled[:, lanes:])):
        out_ref[pl.ds(q, count, stride=4), :] = value


def call(kernel, shape, args, scratch_shapes=(), flops=0, aliases=None, keep=True):
    vmem = pl.BlockSpec(memory_space=pltpu.VMEM)
    specs = [pl.BlockSpec(memory_space=pltpu.SMEM)] + [vmem] * (len(args) - 1)
    args = [args[0]] + [pltpu.with_memory_space_constraint(a, pltpu.VMEM) for a in args[1:]]
    return pl.pallas_call(
        kernel,
        out_shape=pltpu.VMEM(shape, jnp.float32) if keep else jax.ShapeDtypeStruct(shape, jnp.float32),
        in_specs=specs,
        out_specs=vmem,
        scratch_shapes=list(scratch_shapes),
        input_output_aliases=aliases or {},
        cost_estimate=pl.CostEstimate(flops=flops, bytes_accessed=4 * math.prod(shape), transcendentals=0),
        compiler_params=pltpu.CompilerParams(vmem_limit_bytes=24 * 2**20),
    )(*args)


def first_call(rows, place, chunk, field, mask, link, speed, matrix, dtau):
    vmem = pl.BlockSpec(memory_space=pltpu.VMEM)
    given = (mask, link, speed, matrix, dtau)
    sources = [pltpu.with_memory_space_constraint(a, pltpu.HBM) for a in (field, *given)]
    outs = [pltpu.VMEM(a.shape, a.dtype) for a in given] + [pltpu.VMEM((rows, dtau.shape[2]), jnp.float32)]
    return pl.pallas_call(
        first_kernel,
        out_shape=outs,
        in_specs=[pl.BlockSpec(memory_space=pltpu.SMEM)] * 2 + [pl.BlockSpec(memory_space=pltpu.HBM)] * 6,
        out_specs=[vmem] * 6,
        scratch_shapes=[
            *scratch(*mask.shape[1:]),
            pltpu.VMEM(field.shape, jnp.float32),
            pltpu.SemaphoreType.DMA((6,)),
        ],
        cost_estimate=pl.CostEstimate(flops=10**8, bytes_accessed=10**6, transcendentals=0),
        compiler_params=pltpu.CompilerParams(vmem_limit_bytes=24 * 2**20),
    )(place, chunk, *sources)


def shards(matrix, state, frame_velocity, dtau, live_mask, link):
    nj, ni = live_mask.shape[1:]
    flaps, gusts = lax.axis_size("flap"), lax.axis_size("gust")
    count = flaps * gusts
    field = state[0, 0]
    first = jnp.where(lax.axis_index("span") == 0, 1, 0).astype(jnp.int32)[None]
    chunk = (lax.axis_index("flap") * gusts + lax.axis_index("gust")).astype(jnp.int32)[None]
    swap = [(0, 1), (1, 0)]

    def turn(x):
        y = lax.all_to_all(x.reshape(count, 4, ni), ("flap", "gust"), 0, 0, tiled=True)
        return y.reshape(count * 4, ni)

    with jax.named_scope("halo"):
        other = lax.ppermute(field, "span", swap)
    with jax.named_scope("first_divergence"):
        mask, link, speed, matrix, dtau, pack = first_call(
            count * 4, first, chunk, field, live_mask, link[None], frame_velocity[0], matrix, dtau
        )
        pack = call(first_edge_kernel, pack.shape, (first, speed, other, pack), aliases={3: 0})
    with jax.named_scope("turn"):
        pack = turn(pack)
    with jax.named_scope("instances"):
        pack = call(instances_kernel, pack.shape, (chunk, matrix, pack, dtau, mask), (), 10**8)
    with jax.named_scope("turn_back"):
        pack = turn(pack)
    with jax.named_scope("halo"):
        other = lax.ppermute(call(edge_kernel, (5, nj, ni), (first, pack)), "span", swap)
    with jax.named_scope("last_divergence"):
        residual = call(last_kernel, field.shape, (first, speed, pack, mask, link), scratch(nj, ni), 10**8)
        out = call(last_edge_kernel, field.shape, (first, speed, pack, other, residual, mask, dtau), keep=False)
    return out[None, None]


def solution(mesh):
    flap = instance_matrix(mesh.shape["flap"], FLAP_OMEGA)
    gust = instance_matrix(mesh.shape["gust"], GUST_OMEGA)
    matrix = np.kron(flap, np.eye(len(gust))) + np.kron(np.eye(len(flap)), gust)
    matrix = jnp.asarray(matrix.astype(np.float32))
    in_specs = (
        P("flap", "gust", None, "span", None, None),
        P("flap", "gust", None),
        P("span", None, None),
        P("span", None, None),
        P(),
    )
    out_specs = P("flap", "gust", None, "span", None, None)
    return jax.shard_map(
        functools.partial(shards, matrix), mesh=mesh, in_specs=in_specs, out_specs=out_specs, check_vma=False
    )
```

```python
import functools
import math

import jax
import jax.numpy as jnp
import numpy as np
from jax import lax
from jax.experimental import pallas as pl
from jax.experimental.pallas import tpu as pltpu
from jax.sharding import PartitionSpec as P

VISC = 0.12
FLAP_OMEGA = 0.8
GUST_OMEGA = 1.2944

RHO, U, V, W, PR, EN, RT, LIVE = range(8)
PAD = 8


def instance_matrix(count, omega):
    offset = np.arange(count)[:, None] - np.arange(count)[None, :]
    angle = np.pi * offset / count
    parity = np.where(offset % 2 == 0, 1.0, -1.0)
    off = offset != 0
    safe = np.where(off, angle, 0.5 * np.pi)
    first = np.where(off, 0.5 * parity / np.tan(safe), 0.0)
    second = np.where(off, -0.5 * parity / np.sin(safe) ** 2, -(count * count / 12.0 + 1.0 / 6.0))
    return omega * first - VISC * second


def primitives(rho, m1, m2, m3, energy):
    inv = 1.0 / rho
    u, v, w = m1 * inv, m2 * inv, m3 * inv
    p = 0.4 * (energy - 0.5 * (m1 * u + m2 * v + m3 * w))
    return (rho, u, v, w, p, (energy + p) * inv, jnp.sqrt(jnp.abs(rho)))


def physical(cell, axis, g):
    rho, vel, p, enth = cell[RHO], cell[U : W + 1], cell[PR], cell[EN]
    mass = rho * (vel[axis] - g)
    mom = [mass * vel[a] + p if a == axis else mass * vel[a] for a in range(3)]
    return [mass, *mom, mass * enth + g * p]


def roe(left, right, axis, g):
    rho_l, vel_l, p_l, h_l, s_l = left[RHO], left[U : W + 1], left[PR], left[EN], left[RT]
    rho_r, vel_r, p_r, h_r, s_r = right[RHO], right[U : W + 1], right[PR], right[EN], right[RT]
    t1, t2 = [a for a in range(3) if a != axis]
    weight = s_r / (s_l + s_r)
    jump = [vel_r[a] - vel_l[a] for a in range(3)]
    vel = [vel_l[a] + weight * jump[a] for a in range(3)]
    enth = h_l + weight * (h_r - h_l)
    half_sq = 0.5 * (vel[0] * vel[0] + vel[1] * vel[1] + vel[2] * vel[2])
    c_sq = 0.4 * (enth - half_sq)
    inv_c = lax.rsqrt(c_sq)
    c = c_sq * inv_c
    delta = 0.1 * c
    scale = 5.0 * inv_c
    half_inv_sq = 0.5 * (inv_c * inv_c)
    rho_t = s_l * s_r
    dp = p_r - p_l
    drho = rho_r - rho_l
    swing = rho_t * c * jump[axis]

    def speed(value):
        size = jnp.abs(value)
        return jnp.where(size < delta, (value * value + delta * delta) * scale, size)

    rel = vel[axis] - g
    l2 = speed(rel)
    w1 = speed(rel - c) * ((dp - swing) * half_inv_sq)
    w3 = speed(rel + c) * ((dp + swing) * half_inv_sq)
    w2 = l2 * (drho - dp * (2.0 * half_inv_sq))
    shear = l2 * rho_t
    acoustic = w1 + w3
    total = acoustic + w2
    skew = (w3 - w1) * c
    mass_l = rho_l * (vel_l[axis] - g)
    mass_r = rho_r * (vel_r[axis] - g)
    out = [0.5 * (mass_l + mass_r - total)]
    for a in range(3):
        flux = mass_l * vel_l[a] + mass_r * vel_r[a]
        if a == axis:
            flux = flux + (p_l + p_r) - (total * vel[a] + skew)
        else:
            flux = flux - (total * vel[a] + shear * jump[a])
        out.append(0.5 * flux)
    loss = acoustic * enth + w2 * half_sq + skew * vel[axis]
    loss = loss + shear * (vel[t1] * jump[t1] + vel[t2] * jump[t2])
    out.append(0.5 * (mass_l * h_l + mass_r * h_r + g * (p_l + p_r) - loss))
    return out


def walled(left, right, axis):
    live_l, live_r = left[LIVE] > 0.0, right[LIVE] > 0.0
    n = U + axis
    new_l, new_r = [], []
    for f in range(LIVE):
        if f == n:
            new_l.append(jnp.where(live_l, left[f], -right[f]))
            new_r.append(jnp.where(live_r, right[f], -left[f]))
        else:
            new_l.append(jnp.where(live_l, left[f], right[f]))
            new_r.append(jnp.where(live_r, right[f], left[f]))
    return new_l, new_r


def frame(speed_ref, axis):
    return jnp.broadcast_to(speed_ref[:, axis : axis + 1], (8, 128))


def most_of_divergence(load, mask_ref, link_ref, speed_ref, first, cells, faces, emit):
    nj = mask_ref.shape[1]
    blocks = nj // 8
    g0, g1, g2 = [frame(speed_ref, axis) for axis in range(3)]

    def rows(b):
        return pl.multiple_of(8 * b, 8)

    def fill(b, carry):
        row = rows(b)
        for k in range(2):
            values = primitives(*[load(f, k, row) for f in range(5)])
            for f, value in enumerate(values):
                cells[f, k, pl.ds(PAD + row, 8), :] = value
            live = jnp.where(mask_ref[k, pl.ds(row, 8), :] > 0, 1.0, 0.0)
            cells[LIVE, k, pl.ds(PAD + row, 8), :] = live
        return carry

    lax.fori_loop(0, blocks, fill, 0, unroll=True)
    link = jnp.broadcast_to(link_ref[...], (8, link_ref.shape[1]))
    for k in range(2):
        for f in range(8):
            top = cells[f, k, pl.ds(PAD, 8), :]
            below = jnp.take_along_axis(top, link, axis=1)[:1]
            cells[f, k, pl.ds(PAD - 1, 1), :] = below
            last = cells[f, k, pl.ds(PAD + nj - 1, 1), :]
            if f == LIVE:
                last = jnp.ones_like(last)
            cells[f, k, pl.ds(PAD + nj, 8), :] = jnp.broadcast_to(last, (8, last.shape[1]))

    def normal(b, carry):
        row = rows(b)
        for k in range(2):
            left = [cells[f, k, pl.ds(PAD - 1 + row, 8), :] for f in range(8)]
            right = [cells[f, k, pl.ds(PAD + row, 8), :] for f in range(8)]
            flux = roe(*walled(left, right, 1), 1, g1)
            for f in range(5):
                faces[f, k, pl.ds(row, 8), :] = flux[f]
        return carry

    lax.fori_loop(0, blocks + 1, normal, 0, unroll=True)

    def rest(b, carry):
        row = rows(b)
        near = [[cells[f, k, pl.ds(PAD + row, 8), :] for f in range(8)] for k in range(2)]
        inner = roe(near[0], near[1], 2, g2)
        edge = physical([jnp.where(first, near[0][f], near[1][f]) for f in range(7)], 2, g2)
        for k in range(2):
            here = near[k]
            lanes = here[0].shape[1]
            ahead = [pltpu.roll(x, lanes - 1, 1) for x in here]
            chord = roe(*walled(here, ahead, 0), 0, g0)
            for f in range(5):
                after = faces[f, k, pl.ds(row + 1, 8), :] - faces[f, k, pl.ds(row, 8), :]
                after = after + (chord[f] - pltpu.roll(chord[f], 1, 1))
                if k == 0:
                    span = inner[f] - jnp.where(first, edge[f], 0.0)
                else:
                    span = jnp.where(first, 0.0, edge[f]) - inner[f]
                emit(f, k, row, span + after)
        return carry

    lax.fori_loop(0, blocks, rest, 0, unroll=True)


def outer_face(mine, other, speed_ref, first):
    mine, other = primitives(*mine), primitives(*other)
    left = [jnp.where(first, a, b) for a, b in zip(mine, other)]
    right = [jnp.where(first, b, a) for a, b in zip(mine, other)]
    sign = jnp.where(first, 1.0, -1.0)
    return [sign * x for x in roe(left, right, 2, frame(speed_ref, 2))]


def scratch(nj, ni):
    return [
        pltpu.VMEM((8, 2, nj + 2 * PAD, ni), jnp.float32),
        pltpu.VMEM((5, 2, nj + PAD, ni), jnp.float32),
    ]


def packed(f, row, q, nj):
    return pl.ds(4 * (f * nj + row) + q, 8, stride=4)


def first_kernel(place_ref, chunk_ref, *refs):
    sources, targets, (out_ref, cells, faces, state_ref, sems) = refs[:6], refs[6:11], refs[11:]
    mask_ref, link_ref, speed_ref = targets[:3]
    nj = mask_ref.shape[1]
    copies = [
        pltpu.make_async_copy(source, target, sems.at[i])
        for i, (source, target) in enumerate(zip(sources, (state_ref, *targets)))
    ]
    for copy in copies:
        copy.start()
    used = 4 * 5 * nj
    if out_ref.shape[0] > used:
        out_ref[used:, :] = jnp.zeros((out_ref.shape[0] - used, out_ref.shape[1]), jnp.float32)
    for copy in copies[:4]:
        copy.wait()

    def load(f, k, row):
        return state_ref[f, k, pl.ds(row, 8), :]

    def emit(f, k, row, div):
        out_ref[packed(f, row, k, nj), :] = load(f, k, row)
        out_ref[packed(f, row, 2 + k, nj), :] = div

    most_of_divergence(load, mask_ref, link_ref, speed_ref, place_ref[0] > 0, cells, faces, emit)
    for copy in copies[4:]:
        copy.wait()


def first_edge_kernel(place_ref, speed_ref, other_ref, pack_ref, out_ref):
    nj = other_ref.shape[2]
    edge = place_ref[0]
    out_ref[...] = pack_ref[...]
    for row in range(0, nj, 8):
        mine = [pack_ref[packed(f, row, edge, nj), :] for f in range(5)]
        other = [other_ref[f, 1 - edge, pl.ds(row, 8), :] for f in range(5)]
        flux = outer_face(mine, other, speed_ref, edge > 0)
        for f in range(5):
            div = packed(f, row, 2 + edge, nj)
            out_ref[div, :] = pack_ref[div, :] + flux[f]


def last_kernel(place_ref, speed_ref, turned_ref, mask_ref, link_ref, out_ref, cells, faces):
    nj = mask_ref.shape[1]

    def load(f, k, row):
        return turned_ref[packed(f, row, k, nj), :]

    def emit(f, k, row, div):
        out_ref[f, k, pl.ds(row, 8), :] = div + turned_ref[packed(f, row, 2 + k, nj), :]

    most_of_divergence(load, mask_ref, link_ref, speed_ref, place_ref[0] > 0, cells, faces, emit)


def last_edge_kernel(place_ref, speed_ref, turned_ref, other_ref, residual_ref, mask_ref, dtau_ref, out_ref):
    nj = mask_ref.shape[1]
    edge = place_ref[0]
    first = edge > 0
    for row in range(0, nj, 8):
        block = pl.ds(row, 8)
        mine = [turned_ref[packed(f, row, edge, nj), :] for f in range(5)]
        flux = outer_face(mine, [other_ref[f, block, :] for f in range(5)], speed_ref, first)
        for k in (edge, 1 - edge):
            live = mask_ref[k, block, :] > 0
            dtau = dtau_ref[k, block, :]
            for f in range(5):
                residual = residual_ref[f, k, block, :]
                if k is edge:
                    old, residual = mine[f], residual + flux[f]
                else:
                    old = turned_ref[packed(f, row, k, nj), :]
                out_ref[f, k, block, :] = jnp.where(live, old - dtau * residual, old)


def edge_kernel(place_ref, turned_ref, out_ref):
    nj = out_ref.shape[1]
    for f in range(5):
        for row in range(0, nj, 8):
            out_ref[f, pl.ds(row, 8), :] = turned_ref[packed(f, row, place_ref[0], nj), :]


def instances_kernel(chunk_ref, matrix_ref, turned_ref, dtau_ref, mask_ref, out_ref):
    count = matrix_ref.shape[0]
    nj = mask_ref.shape[1]
    j = lax.rem(chunk_ref[0], nj)
    parts = [turned_ref[pl.ds(q, count, stride=4), :] for q in range(4)]
    state = jnp.concatenate(parts[:2], axis=1)
    div = jnp.concatenate(parts[2:], axis=1)
    dtau = jnp.concatenate([dtau_ref[k, pl.ds(j, 1), :] for k in range(2)], axis=1)
    mask = jnp.concatenate([mask_ref[k, pl.ds(j, 1), :] for k in range(2)], axis=1)
    matrix = matrix_ref[...]

    def times(x):
        return jnp.dot(matrix, x, precision=lax.Precision.HIGH, preferred_element_type=jnp.float32)

    new = state - dtau * (div + times(state))
    new = jnp.where(mask > 0, new, state)
    coupled = times(new)
    lanes = dtau_ref.shape[2]
    for q, value in enumerate((new[:, :lanes], new[:, lanes:], coupled[:, :lanes], coupled[:, lanes:])):
        out_ref[pl.ds(q, count, stride=4), :] = value


def call(kernel, shape, args, scratch_shapes=(), flops=0, aliases=None, keep=True):
    vmem = pl.BlockSpec(memory_space=pltpu.VMEM)
    specs = [pl.BlockSpec(memory_space=pltpu.SMEM)] + [vmem] * (len(args) - 1)
    args = [args[0]] + [pltpu.with_memory_space_constraint(a, pltpu.VMEM) for a in args[1:]]
    return pl.pallas_call(
        kernel,
        out_shape=pltpu.VMEM(shape, jnp.float32) if keep else jax.ShapeDtypeStruct(shape, jnp.float32),
        in_specs=specs,
        out_specs=vmem,
        scratch_shapes=list(scratch_shapes),
        input_output_aliases=aliases or {},
        cost_estimate=pl.CostEstimate(flops=flops, bytes_accessed=4 * math.prod(shape), transcendentals=0),
        compiler_params=pltpu.CompilerParams(vmem_limit_bytes=24 * 2**20),
    )(*args)


def first_call(rows, place, chunk, field, mask, link, speed, matrix, dtau):
    vmem = pl.BlockSpec(memory_space=pltpu.VMEM)
    given = (mask, link, speed, matrix, dtau)
    sources = [pltpu.with_memory_space_constraint(a, pltpu.HBM) for a in (field, *given)]
    outs = [pltpu.VMEM(a.shape, a.dtype) for a in given] + [pltpu.VMEM((rows, dtau.shape[2]), jnp.float32)]
    return pl.pallas_call(
        first_kernel,
        out_shape=outs,
        in_specs=[pl.BlockSpec(memory_space=pltpu.SMEM)] * 2 + [pl.BlockSpec(memory_space=pltpu.HBM)] * 6,
        out_specs=[vmem] * 6,
        scratch_shapes=[
            *scratch(*mask.shape[1:]),
            pltpu.VMEM(field.shape, jnp.float32),
            pltpu.SemaphoreType.DMA((6,)),
        ],
        cost_estimate=pl.CostEstimate(flops=10**8, bytes_accessed=10**6, transcendentals=0),
        compiler_params=pltpu.CompilerParams(vmem_limit_bytes=24 * 2**20),
    )(place, chunk, *sources)


def shards(matrix, state, frame_velocity, dtau, live_mask, link):
    nj, ni = live_mask.shape[1:]
    flaps, gusts = lax.axis_size("flap"), lax.axis_size("gust")
    count = flaps * gusts
    field = state[0, 0]
    first = jnp.where(lax.axis_index("span") == 0, 1, 0).astype(jnp.int32)[None]
    chunk = (lax.axis_index("flap") * gusts + lax.axis_index("gust")).astype(jnp.int32)[None]
    swap = [(0, 1), (1, 0)]

    def turn(x):
        y = lax.all_to_all(x.reshape(count, 4, ni), ("flap", "gust"), 0, 0, tiled=True)
        return y.reshape(count * 4, ni)

    with jax.named_scope("halo"):
        other = lax.ppermute(field, "span", swap)
    with jax.named_scope("first_divergence"):
        mask, link, speed, matrix, dtau, pack = first_call(
            count * 4, first, chunk, field, live_mask, link[None], frame_velocity[0], matrix, dtau
        )
        pack = call(first_edge_kernel, pack.shape, (first, speed, other, pack), aliases={3: 0})
    with jax.named_scope("turn"):
        pack = turn(pack)
    with jax.named_scope("instances"):
        pack = call(instances_kernel, pack.shape, (chunk, matrix, pack, dtau, mask), (), 10**8)
    with jax.named_scope("turn_back"):
        pack = turn(pack)
    with jax.named_scope("halo"):
        other = lax.ppermute(call(edge_kernel, (5, nj, ni), (first, pack)), "span", swap)
    with jax.named_scope("last_divergence"):
        residual = call(last_kernel, field.shape, (first, speed, pack, mask, link), scratch(nj, ni), 10**8)
        out = call(last_edge_kernel, field.shape, (first, speed, pack, other, residual, mask, dtau), keep=False)
    return out[None, None]


def solution(mesh):
    flap = instance_matrix(mesh.shape["flap"], FLAP_OMEGA)
    gust = instance_matrix(mesh.shape["gust"], GUST_OMEGA)
    matrix = np.kron(flap, np.eye(len(gust))) + np.kron(np.eye(len(flap)), gust)
    matrix = jnp.asarray(matrix.astype(np.float32))
    in_specs = (
        P("flap", "gust", None, "span", None, None),
        P("flap", "gust", None),
        P("span", None, None),
        P("span", None, None),
        P(),
    )
    out_specs = P("flap", "gust", None, "span", None, None)
    return jax.shard_map(
        functools.partial(shards, matrix), mesh=mesh, in_specs=in_specs, out_specs=out_specs, check_vma=False
    )
```

```python
import functools
import math

import jax
import jax.numpy as jnp
import numpy as np
from jax import lax
from jax.experimental import pallas as pl
from jax.experimental.pallas import tpu as pltpu
from jax.sharding import PartitionSpec as P

VISC = 0.12
FLAP_OMEGA = 0.8
GUST_OMEGA = 1.2944

RHO, U, V, W, PR, EN, RT, LIVE = range(8)
PAD = 8


def instance_matrix(count, omega):
    offset = np.arange(count)[:, None] - np.arange(count)[None, :]
    angle = np.pi * offset / count
    parity = np.where(offset % 2 == 0, 1.0, -1.0)
    off = offset != 0
    safe = np.where(off, angle, 0.5 * np.pi)
    first = np.where(off, 0.5 * parity / np.tan(safe), 0.0)
    second = np.where(off, -0.5 * parity / np.sin(safe) ** 2, -(count * count / 12.0 + 1.0 / 6.0))
    return omega * first - VISC * second


def primitives(rho, m1, m2, m3, energy):
    inv = 1.0 / rho
    u, v, w = m1 * inv, m2 * inv, m3 * inv
    p = 0.4 * (energy - 0.5 * (m1 * u + m2 * v + m3 * w))
    return (rho, u, v, w, p, (energy + p) * inv, jnp.sqrt(jnp.abs(rho)))


def physical(cell, axis, g):
    rho, vel, p, enth = cell[RHO], cell[U : W + 1], cell[PR], cell[EN]
    mass = rho * (vel[axis] - g)
    mom = [mass * vel[a] + p if a == axis else mass * vel[a] for a in range(3)]
    return [mass, *mom, mass * enth + g * p]


def roe(left, right, axis, g):
    rho_l, vel_l, p_l, h_l, s_l = left[RHO], left[U : W + 1], left[PR], left[EN], left[RT]
    rho_r, vel_r, p_r, h_r, s_r = right[RHO], right[U : W + 1], right[PR], right[EN], right[RT]
    t1, t2 = [a for a in range(3) if a != axis]
    weight = s_r / (s_l + s_r)
    jump = [vel_r[a] - vel_l[a] for a in range(3)]
    vel = [vel_l[a] + weight * jump[a] for a in range(3)]
    enth = h_l + weight * (h_r - h_l)
    half_sq = 0.5 * (vel[0] * vel[0] + vel[1] * vel[1] + vel[2] * vel[2])
    c_sq = 0.4 * (enth - half_sq)
    inv_c = lax.rsqrt(c_sq)
    c = c_sq * inv_c
    delta = 0.1 * c
    scale = 5.0 * inv_c
    half_inv_sq = 0.5 * (inv_c * inv_c)
    rho_t = s_l * s_r
    dp = p_r - p_l
    drho = rho_r - rho_l
    swing = rho_t * c * jump[axis]

    def speed(value):
        size = jnp.abs(value)
        return jnp.where(size < delta, (value * value + delta * delta) * scale, size)

    rel = vel[axis] - g
    l2 = speed(rel)
    w1 = speed(rel - c) * ((dp - swing) * half_inv_sq)
    w3 = speed(rel + c) * ((dp + swing) * half_inv_sq)
    w2 = l2 * (drho - dp * (2.0 * half_inv_sq))
    shear = l2 * rho_t
    acoustic = w1 + w3
    total = acoustic + w2
    skew = (w3 - w1) * c
    mass_l = rho_l * (vel_l[axis] - g)
    mass_r = rho_r * (vel_r[axis] - g)
    out = [0.5 * (mass_l + mass_r - total)]
    for a in range(3):
        flux = mass_l * vel_l[a] + mass_r * vel_r[a]
        if a == axis:
            flux = flux + (p_l + p_r) - (total * vel[a] + skew)
        else:
            flux = flux - (total * vel[a] + shear * jump[a])
        out.append(0.5 * flux)
    loss = acoustic * enth + w2 * half_sq + skew * vel[axis]
    loss = loss + shear * (vel[t1] * jump[t1] + vel[t2] * jump[t2])
    out.append(0.5 * (mass_l * h_l + mass_r * h_r + g * (p_l + p_r) - loss))
    return out


def walled(left, right, axis):
    live_l, live_r = left[LIVE] > 0.0, right[LIVE] > 0.0
    n = U + axis
    new_l, new_r = [], []
    for f in range(LIVE):
        if f == n:
            new_l.append(jnp.where(live_l, left[f], -right[f]))
            new_r.append(jnp.where(live_r, right[f], -left[f]))
        else:
            new_l.append(jnp.where(live_l, left[f], right[f]))
            new_r.append(jnp.where(live_r, right[f], left[f]))
    return new_l, new_r


def frame(speed_ref, axis):
    return jnp.broadcast_to(speed_ref[:, axis : axis + 1], (8, 128))


def most_of_divergence(load, mask_ref, link_ref, speed_ref, first, cells, faces, emit):
    nj = mask_ref.shape[1]
    blocks = nj // 8
    g0, g1, g2 = [frame(speed_ref, axis) for axis in range(3)]

    def rows(b):
        return pl.multiple_of(8 * b, 8)

    def fill(b, carry):
        row = rows(b)
        for k in range(2):
            values = primitives(*[load(f, k, row) for f in range(5)])
            for f, value in enumerate(values):
                cells[f, k, pl.ds(PAD + row, 8), :] = value
            live = jnp.where(mask_ref[k, pl.ds(row, 8), :] > 0, 1.0, 0.0)
            cells[LIVE, k, pl.ds(PAD + row, 8), :] = live
        return carry

    lax.fori_loop(0, blocks, fill, 0, unroll=True)
    link = jnp.broadcast_to(link_ref[...], (8, link_ref.shape[1]))
    for k in range(2):
        for f in range(8):
            top = cells[f, k, pl.ds(PAD, 8), :]
            below = jnp.take_along_axis(top, link, axis=1)[:1]
            cells[f, k, pl.ds(PAD - 1, 1), :] = below
            last = cells[f, k, pl.ds(PAD + nj - 1, 1), :]
            if f == LIVE:
                last = jnp.ones_like(last)
            cells[f, k, pl.ds(PAD + nj, 8), :] = jnp.broadcast_to(last, (8, last.shape[1]))

    def normal(b, carry):
        row = rows(b)
        for k in range(2):
            left = [cells[f, k, pl.ds(PAD - 1 + row, 8), :] for f in range(8)]
            right = [cells[f, k, pl.ds(PAD + row, 8), :] for f in range(8)]
            flux = roe(*walled(left, right, 1), 1, g1)
            for f in range(5):
                faces[f, k, pl.ds(row, 8), :] = flux[f]
        return carry

    lax.fori_loop(0, blocks + 1, normal, 0, unroll=True)

    def rest(b, carry):
        row = rows(b)
        near = [[cells[f, k, pl.ds(PAD + row, 8), :] for f in range(8)] for k in range(2)]
        inner = roe(near[0], near[1], 2, g2)
        edge = physical([jnp.where(first, near[0][f], near[1][f]) for f in range(7)], 2, g2)
        for k in range(2):
            here = near[k]
            lanes = here[0].shape[1]
            ahead = [pltpu.roll(x, lanes - 1, 1) for x in here]
            chord = roe(*walled(here, ahead, 0), 0, g0)
            for f in range(5):
                after = faces[f, k, pl.ds(row + 1, 8), :] - faces[f, k, pl.ds(row, 8), :]
                after = after + (chord[f] - pltpu.roll(chord[f], 1, 1))
                if k == 0:
                    span = inner[f] - jnp.where(first, edge[f], 0.0)
                else:
                    span = jnp.where(first, 0.0, edge[f]) - inner[f]
                emit(f, k, row, span + after)
        return carry

    lax.fori_loop(0, blocks, rest, 0, unroll=True)


def outer_face(mine, other, speed_ref, first):
    other = primitives(*other)
    left = [jnp.where(first, a, b) for a, b in zip(mine, other)]
    right = [jnp.where(first, b, a) for a, b in zip(mine, other)]
    sign = jnp.where(first, 1.0, -1.0)
    return [sign * x for x in roe(left, right, 2, frame(speed_ref, 2))]


def scratch(nj, ni):
    return [
        pltpu.VMEM((8, 2, nj + 2 * PAD, ni), jnp.float32),
        pltpu.VMEM((5, 2, nj + PAD, ni), jnp.float32),
    ]


def packed(f, row, q, nj):
    return pl.ds(4 * (f * nj + row) + q, 8, stride=4)


def first_kernel(place_ref, chunk_ref, *refs):
    sources, targets, (out_ref, near_ref, cells, faces, state_ref, sems) = refs[:6], refs[6:11], refs[11:]
    mask_ref, link_ref, speed_ref = targets[:3]
    nj = mask_ref.shape[1]
    copies = [
        pltpu.make_async_copy(source, target, sems.at[i])
        for i, (source, target) in enumerate(zip(sources, (state_ref, *targets)))
    ]
    for copy in copies:
        copy.start()
    used = 4 * 5 * nj
    if out_ref.shape[0] > used:
        out_ref[used:, :] = jnp.zeros((out_ref.shape[0] - used, out_ref.shape[1]), jnp.float32)
    for copy in copies[:4]:
        copy.wait()

    def load(f, k, row):
        return state_ref[f, k, pl.ds(row, 8), :]

    def emit(f, k, row, div):
        out_ref[packed(f, row, k, nj), :] = load(f, k, row)
        out_ref[packed(f, row, 2 + k, nj), :] = div

    most_of_divergence(load, mask_ref, link_ref, speed_ref, place_ref[0] > 0, cells, faces, emit)
    near_ref[...] = cells[:LIVE, place_ref[0], PAD : PAD + nj, :]
    for copy in copies[4:]:
        copy.wait()


def first_edge_kernel(place_ref, speed_ref, near_ref, other_ref, pack_ref, out_ref):
    nj = other_ref.shape[2]
    edge = place_ref[0]
    out_ref[...] = pack_ref[...]
    for row in range(0, nj, 8):
        mine = [near_ref[f, pl.ds(row, 8), :] for f in range(LIVE)]
        other = [other_ref[f, 1 - edge, pl.ds(row, 8), :] for f in range(5)]
        flux = outer_face(mine, other, speed_ref, edge > 0)
        for f in range(5):
            div = packed(f, row, 2 + edge, nj)
            out_ref[div, :] = pack_ref[div, :] + flux[f]


def last_kernel(place_ref, speed_ref, turned_ref, mask_ref, dtau_ref, link_ref, out_ref, near_ref, cells, faces):
    nj = mask_ref.shape[1]

    def load(f, k, row):
        return turned_ref[packed(f, row, k, nj), :]

    def emit(f, k, row, div):
        block = pl.ds(row, 8)
        old = load(f, k, row)
        new = old - dtau_ref[k, block, :] * (div + turned_ref[packed(f, row, 2 + k, nj), :])
        out_ref[f, k, block, :] = jnp.where(mask_ref[k, block, :] > 0, new, old)

    most_of_divergence(load, mask_ref, link_ref, speed_ref, place_ref[0] > 0, cells, faces, emit)
    near_ref[...] = cells[:LIVE, place_ref[0], PAD : PAD + nj, :]


def last_edge_kernel(place_ref, speed_ref, near_ref, other_ref, most_ref, mask_ref, dtau_ref, out_ref):
    nj = mask_ref.shape[1]
    edge = place_ref[0]
    for f in range(5):
        out_ref[f, 1 - edge, :, :] = most_ref[f, 1 - edge, :, :]
    for row in range(0, nj, 8):
        block = pl.ds(row, 8)
        mine = [near_ref[f, block, :] for f in range(LIVE)]
        flux = outer_face(mine, [other_ref[f, block, :] for f in range(5)], speed_ref, edge > 0)
        live = mask_ref[edge, block, :] > 0
        dtau = dtau_ref[edge, block, :]
        for f in range(5):
            most = most_ref[f, edge, block, :]
            out_ref[f, edge, block, :] = jnp.where(live, most - dtau * flux[f], most)


def edge_kernel(place_ref, turned_ref, out_ref):
    nj = out_ref.shape[1]
    for f in range(5):
        for row in range(0, nj, 8):
            out_ref[f, pl.ds(row, 8), :] = turned_ref[packed(f, row, place_ref[0], nj), :]


def instances_kernel(chunk_ref, matrix_ref, turned_ref, dtau_ref, mask_ref, out_ref):
    count = matrix_ref.shape[0]
    nj = mask_ref.shape[1]
    j = lax.rem(chunk_ref[0], nj)
    parts = [turned_ref[pl.ds(q, count, stride=4), :] for q in range(4)]
    state = jnp.concatenate(parts[:2], axis=1)
    div = jnp.concatenate(parts[2:], axis=1)
    dtau = jnp.concatenate([dtau_ref[k, pl.ds(j, 1), :] for k in range(2)], axis=1)
    mask = jnp.concatenate([mask_ref[k, pl.ds(j, 1), :] for k in range(2)], axis=1)
    matrix = matrix_ref[...]

    def times(x):
        return jnp.dot(matrix, x, precision=lax.Precision.HIGH, preferred_element_type=jnp.float32)

    new = state - dtau * (div + times(state))
    new = jnp.where(mask > 0, new, state)
    coupled = times(new)
    lanes = dtau_ref.shape[2]
    for q, value in enumerate((new[:, :lanes], new[:, lanes:], coupled[:, :lanes], coupled[:, lanes:])):
        out_ref[pl.ds(q, count, stride=4), :] = value


def call(kernel, shapes, args, scratch_shapes=(), flops=0, aliases=None, keep=True):
    vmem = pl.BlockSpec(memory_space=pltpu.VMEM)
    specs = [pl.BlockSpec(memory_space=pltpu.SMEM)] + [vmem] * (len(args) - 1)
    args = [args[0]] + [pltpu.with_memory_space_constraint(a, pltpu.VMEM) for a in args[1:]]
    held = pltpu.VMEM if keep else jax.ShapeDtypeStruct
    outs = pl.pallas_call(
        kernel,
        out_shape=[held(shape, jnp.float32) for shape in shapes],
        in_specs=specs,
        out_specs=[vmem] * len(shapes),
        scratch_shapes=list(scratch_shapes),
        input_output_aliases=aliases or {},
        cost_estimate=pl.CostEstimate(flops=flops, bytes_accessed=10**6, transcendentals=0),
        compiler_params=pltpu.CompilerParams(vmem_limit_bytes=24 * 2**20),
    )(*args)
    return outs if len(shapes) > 1 else outs[0]


def first_call(rows, place, chunk, field, mask, link, speed, matrix, dtau):
    vmem = pl.BlockSpec(memory_space=pltpu.VMEM)
    nj, ni = mask.shape[1:]
    given = (mask, link, speed, matrix, dtau)
    sources = [pltpu.with_memory_space_constraint(a, pltpu.HBM) for a in (field, *given)]
    outs = [pltpu.VMEM(a.shape, a.dtype) for a in given]
    outs += [pltpu.VMEM(shape, jnp.float32) for shape in ((rows, ni), (LIVE, nj, ni))]
    return pl.pallas_call(
        first_kernel,
        out_shape=outs,
        in_specs=[pl.BlockSpec(memory_space=pltpu.SMEM)] * 2 + [pl.BlockSpec(memory_space=pltpu.HBM)] * 6,
        out_specs=[vmem] * 7,
        scratch_shapes=[*scratch(nj, ni), pltpu.VMEM(field.shape, jnp.float32), pltpu.SemaphoreType.DMA((6,))],
        cost_estimate=pl.CostEstimate(flops=10**8, bytes_accessed=10**6, transcendentals=0),
        compiler_params=pltpu.CompilerParams(vmem_limit_bytes=24 * 2**20),
    )(place, chunk, *sources)


def shards(matrix, state, frame_velocity, dtau, live_mask, link):
    nj, ni = live_mask.shape[1:]
    flaps, gusts = lax.axis_size("flap"), lax.axis_size("gust")
    count = flaps * gusts
    field = state[0, 0]
    first = jnp.where(lax.axis_index("span") == 0, 1, 0).astype(jnp.int32)[None]
    chunk = (lax.axis_index("flap") * gusts + lax.axis_index("gust")).astype(jnp.int32)[None]
    swap = [(0, 1), (1, 0)]

    def turn(x):
        y = lax.all_to_all(x.reshape(count, 4, ni), ("flap", "gust"), 0, 0, tiled=True)
        return y.reshape(count * 4, ni)

    with jax.named_scope("halo"):
        other = lax.ppermute(field, "span", swap)
    with jax.named_scope("first_divergence"):
        mask, link, speed, matrix, dtau, pack, near = first_call(
            count * 4, first, chunk, field, live_mask, link[None], frame_velocity[0], matrix, dtau
        )
        pack = call(first_edge_kernel, [pack.shape], (first, speed, near, other, pack), aliases={4: 0})
    with jax.named_scope("turn"):
        pack = turn(pack)
    with jax.named_scope("instances"):
        pack = call(instances_kernel, [pack.shape], (chunk, matrix, pack, dtau, mask), (), 10**8)
    with jax.named_scope("turn_back"):
        pack = turn(pack)
    with jax.named_scope("halo"):
        other = lax.ppermute(call(edge_kernel, [(5, nj, ni)], (first, pack)), "span", swap)
    with jax.named_scope("last_divergence"):
        most, near = call(
            last_kernel,
            [field.shape, (LIVE, nj, ni)],
            (first, speed, pack, mask, dtau, link),
            scratch(nj, ni),
            10**8,
        )
        out = call(last_edge_kernel, [field.shape], (first, speed, near, other, most, mask, dtau), keep=False)
    return out[None, None]


def solution(mesh):
    flap = instance_matrix(mesh.shape["flap"], FLAP_OMEGA)
    gust = instance_matrix(mesh.shape["gust"], GUST_OMEGA)
    matrix = np.kron(flap, np.eye(len(gust))) + np.kron(np.eye(len(flap)), gust)
    matrix = jnp.asarray(matrix.astype(np.float32))
    in_specs = (
        P("flap", "gust", None, "span", None, None),
        P("flap", "gust", None),
        P("span", None, None),
        P("span", None, None),
        P(),
    )
    out_specs = P("flap", "gust", None, "span", None, None)
    return jax.shard_map(
        functools.partial(shards, matrix), mesh=mesh, in_specs=in_specs, out_specs=out_specs, check_vma=False
    )
```

```python
import functools
import math

import jax
import jax.numpy as jnp
import numpy as np
from jax import lax
from jax.experimental import pallas as pl
from jax.experimental.pallas import tpu as pltpu
from jax.sharding import PartitionSpec as P

VISC = 0.12
FLAP_OMEGA = 0.8
GUST_OMEGA = 1.2944

RHO, U, V, W, PR, EN, RT, LIVE = range(8)
PAD = 8


def instance_matrix(count, omega):
    offset = np.arange(count)[:, None] - np.arange(count)[None, :]
    angle = np.pi * offset / count
    parity = np.where(offset % 2 == 0, 1.0, -1.0)
    off = offset != 0
    safe = np.where(off, angle, 0.5 * np.pi)
    first = np.where(off, 0.5 * parity / np.tan(safe), 0.0)
    second = np.where(off, -0.5 * parity / np.sin(safe) ** 2, -(count * count / 12.0 + 1.0 / 6.0))
    return omega * first - VISC * second


def primitives(rho, m1, m2, m3, energy):
    inv = 1.0 / rho
    u, v, w = m1 * inv, m2 * inv, m3 * inv
    p = 0.4 * (energy - 0.5 * (m1 * u + m2 * v + m3 * w))
    return (rho, u, v, w, p, (energy + p) * inv, jnp.sqrt(jnp.abs(rho)))


def physical(cell, axis, g):
    rho, vel, p, enth = 2.0 * cell[RHO], cell[U : W + 1], 2.0 * cell[PR], cell[EN]
    mass = rho * (vel[axis] - g)
    mom = [mass * vel[a] + p if a == axis else mass * vel[a] for a in range(3)]
    return [mass, *mom, mass * enth + g * p]


def roe(left, right, axis, g):
    rho_l, vel_l, p_l, h_l, s_l = left[RHO], left[U : W + 1], left[PR], left[EN], left[RT]
    rho_r, vel_r, p_r, h_r, s_r = right[RHO], right[U : W + 1], right[PR], right[EN], right[RT]
    t1, t2 = [a for a in range(3) if a != axis]
    weight = s_r / (s_l + s_r)
    jump = [vel_r[a] - vel_l[a] for a in range(3)]
    vel = [vel_l[a] + weight * jump[a] for a in range(3)]
    enth = h_l + weight * (h_r - h_l)
    half_sq = 0.5 * (vel[0] * vel[0] + vel[1] * vel[1] + vel[2] * vel[2])
    c_sq = 0.4 * (enth - half_sq)
    inv_c = lax.rsqrt(c_sq)
    c = c_sq * inv_c
    delta = 0.1 * c
    scale = 5.0 * inv_c
    half_inv_sq = 0.5 * (inv_c * inv_c)
    rho_t = s_l * s_r
    dp = p_r - p_l
    drho = rho_r - rho_l
    swing = rho_t * c * jump[axis]

    def speed(value):
        size = jnp.abs(value)
        return jnp.where(size < delta, (value * value + delta * delta) * scale, size)

    rel = vel[axis] - g
    l2 = speed(rel)
    w1 = speed(rel - c) * ((dp - swing) * half_inv_sq)
    w3 = speed(rel + c) * ((dp + swing) * half_inv_sq)
    w2 = l2 * (drho - dp * (2.0 * half_inv_sq))
    shear = l2 * rho_t
    acoustic = w1 + w3
    total = acoustic + w2
    skew = (w3 - w1) * c
    mass_l = rho_l * (vel_l[axis] - g)
    mass_r = rho_r * (vel_r[axis] - g)
    out = [mass_l + mass_r - total]
    for a in range(3):
        flux = mass_l * vel_l[a] + mass_r * vel_r[a]
        if a == axis:
            flux = flux + (p_l + p_r) - (total * vel[a] + skew)
        else:
            flux = flux - (total * vel[a] + shear * jump[a])
        out.append(flux)
    loss = acoustic * enth + w2 * half_sq + skew * vel[axis]
    loss = loss + shear * (vel[t1] * jump[t1] + vel[t2] * jump[t2])
    out.append(mass_l * h_l + mass_r * h_r + g * (p_l + p_r) - loss)
    return out


def walled(left, right, axis):
    live_l, live_r = left[LIVE] > 0.0, right[LIVE] > 0.0
    n = U + axis
    new_l, new_r = [], []
    for f in range(LIVE):
        if f == n:
            new_l.append(jnp.where(live_l, left[f], -right[f]))
            new_r.append(jnp.where(live_r, right[f], -left[f]))
        else:
            new_l.append(jnp.where(live_l, left[f], right[f]))
            new_r.append(jnp.where(live_r, right[f], left[f]))
    return new_l, new_r


def frame(speed_ref, axis):
    return jnp.broadcast_to(speed_ref[:, axis : axis + 1], (8, 128))


def most_of_divergence(load, mask_ref, link_ref, speed_ref, first, cells, faces, emit):
    nj = mask_ref.shape[1]
    blocks = nj // 8
    g0, g1, g2 = [frame(speed_ref, axis) for axis in range(3)]

    def rows(b):
        return pl.multiple_of(8 * b, 8)

    def fill(b, carry):
        row = rows(b)
        for k in range(2):
            values = primitives(*[load(f, k, row) for f in range(5)])
            for f, value in enumerate(values):
                cells[f, k, pl.ds(PAD + row, 8), :] = value
            live = jnp.where(mask_ref[k, pl.ds(row, 8), :] > 0, 1.0, 0.0)
            cells[LIVE, k, pl.ds(PAD + row, 8), :] = live
        return carry

    lax.fori_loop(0, blocks, fill, 0, unroll=True)
    link = jnp.broadcast_to(link_ref[...], (8, link_ref.shape[1]))
    for k in range(2):
        for f in range(8):
            top = cells[f, k, pl.ds(PAD, 8), :]
            below = jnp.take_along_axis(top, link, axis=1)[:1]
            cells[f, k, pl.ds(PAD - 1, 1), :] = below
            last = cells[f, k, pl.ds(PAD + nj - 1, 1), :]
            if f == LIVE:
                last = jnp.ones_like(last)
            cells[f, k, pl.ds(PAD + nj, 8), :] = jnp.broadcast_to(last, (8, last.shape[1]))

    def normal(b, carry):
        row = rows(b)
        for k in range(2):
            left = [cells[f, k, pl.ds(PAD - 1 + row, 8), :] for f in range(8)]
            right = [cells[f, k, pl.ds(PAD + row, 8), :] for f in range(8)]
            flux = roe(*walled(left, right, 1), 1, g1)
            for f in range(5):
                faces[f, k, pl.ds(row, 8), :] = flux[f]
        return carry

    lax.fori_loop(0, blocks + 1, normal, 0, unroll=True)

    def rest(b, carry):
        row = rows(b)
        near = [[cells[f, k, pl.ds(PAD + row, 8), :] for f in range(8)] for k in range(2)]
        inner = roe(near[0], near[1], 2, g2)
        edge = physical([jnp.where(first, near[0][f], near[1][f]) for f in range(7)], 2, g2)
        for k in range(2):
            here = near[k]
            lanes = here[0].shape[1]
            ahead = [pltpu.roll(x, lanes - 1, 1) for x in here]
            chord = roe(*walled(here, ahead, 0), 0, g0)
            for f in range(5):
                after = faces[f, k, pl.ds(row + 1, 8), :] - faces[f, k, pl.ds(row, 8), :]
                after = after + (chord[f] - pltpu.roll(chord[f], 1, 1))
                if k == 0:
                    span = inner[f] - jnp.where(first, edge[f], 0.0)
                else:
                    span = jnp.where(first, 0.0, edge[f]) - inner[f]
                emit(f, k, row, 0.5 * (span + after))
        return carry

    lax.fori_loop(0, blocks, rest, 0, unroll=True)


def outer_face(mine, other, speed_ref, first):
    other = primitives(*other)
    left = [jnp.where(first, a, b) for a, b in zip(mine, other)]
    right = [jnp.where(first, b, a) for a, b in zip(mine, other)]
    sign = jnp.where(first, 0.5, -0.5)
    return [sign * x for x in roe(left, right, 2, frame(speed_ref, 2))]


def scratch(nj, ni):
    return [
        pltpu.VMEM((8, 2, nj + 2 * PAD, ni), jnp.float32),
        pltpu.VMEM((5, 2, nj + PAD, ni), jnp.float32),
    ]


def packed(f, row, q, nj):
    return pl.ds(4 * (f * nj + row) + q, 8, stride=4)


def first_kernel(place_ref, chunk_ref, *refs):
    sources, targets, (out_ref, near_ref, cells, faces, sems) = refs[:6], refs[6:12], refs[12:]
    state_ref, mask_ref, link_ref, speed_ref = targets[:4]
    nj = mask_ref.shape[1]
    copies = [
        pltpu.make_async_copy(source, target, sems.at[i])
        for i, (source, target) in enumerate(zip(sources, targets))
    ]
    for copy in copies:
        copy.start()
    for copy in copies[:4]:
        copy.wait()

    def load(f, k, row):
        return state_ref[f, k, pl.ds(row, 8), :]

    def emit(f, k, row, div):
        out_ref[f, k, pl.ds(row, 8), :] = div

    most_of_divergence(load, mask_ref, link_ref, speed_ref, place_ref[0] > 0, cells, faces, emit)
    near_ref[...] = cells[:LIVE, place_ref[0], PAD : PAD + nj, :]
    for copy in copies[4:]:
        copy.wait()


def first_edge_kernel(place_ref, speed_ref, near_ref, other_ref, state_ref, div_ref, out_ref):
    nj = other_ref.shape[2]
    edge = place_ref[0]
    used = 4 * 5 * nj
    if out_ref.shape[0] > used:
        out_ref[used:, :] = jnp.zeros((out_ref.shape[0] - used, out_ref.shape[1]), jnp.float32)
    for row in range(0, nj, 8):
        block = pl.ds(row, 8)
        mine = [near_ref[f, block, :] for f in range(LIVE)]
        other = [other_ref[f, 1 - edge, block, :] for f in range(5)]
        flux = outer_face(mine, other, speed_ref, edge > 0)
        for f in range(5):
            for k in range(2):
                out_ref[packed(f, row, k, nj), :] = state_ref[f, k, block, :]
            out_ref[packed(f, row, 2 + edge, nj), :] = div_ref[f, edge, block, :] + flux[f]
            out_ref[packed(f, row, 3 - edge, nj), :] = div_ref[f, 1 - edge, block, :]


def last_kernel(place_ref, speed_ref, turned_ref, mask_ref, dtau_ref, link_ref, out_ref, near_ref, cells, faces):
    nj = mask_ref.shape[1]

    def load(f, k, row):
        return turned_ref[packed(f, row, k, nj), :]

    def emit(f, k, row, div):
        block = pl.ds(row, 8)
        old = load(f, k, row)
        new = old - dtau_ref[k, block, :] * (div + turned_ref[packed(f, row, 2 + k, nj), :])
        out_ref[f, k, block, :] = jnp.where(mask_ref[k, block, :] > 0, new, old)

    most_of_divergence(load, mask_ref, link_ref, speed_ref, place_ref[0] > 0, cells, faces, emit)
    near_ref[...] = cells[:LIVE, place_ref[0], PAD : PAD + nj, :]


def last_edge_kernel(place_ref, speed_ref, near_ref, other_ref, most_ref, mask_ref, dtau_ref, out_ref):
    nj = mask_ref.shape[1]
    edge = place_ref[0]
    for f in range(5):
        out_ref[f, 1 - edge, :, :] = most_ref[f, 1 - edge, :, :]
    for row in range(0, nj, 8):
        block = pl.ds(row, 8)
        mine = [near_ref[f, block, :] for f in range(LIVE)]
        flux = outer_face(mine, [other_ref[f, block, :] for f in range(5)], speed_ref, edge > 0)
        live = mask_ref[edge, block, :] > 0
        dtau = dtau_ref[edge, block, :]
        for f in range(5):
            most = most_ref[f, edge, block, :]
            out_ref[f, edge, block, :] = jnp.where(live, most - dtau * flux[f], most)


def edge_kernel(place_ref, turned_ref, out_ref):
    nj = out_ref.shape[1]
    for f in range(5):
        for row in range(0, nj, 8):
            out_ref[f, pl.ds(row, 8), :] = turned_ref[packed(f, row, place_ref[0], nj), :]


def instances_kernel(chunk_ref, matrix_ref, turned_ref, dtau_ref, mask_ref, out_ref):
    count = matrix_ref.shape[0]
    nj = mask_ref.shape[1]
    j = lax.rem(chunk_ref[0], nj)
    parts = [turned_ref[pl.ds(q, count, stride=4), :] for q in range(4)]
    state = jnp.concatenate(parts[:2], axis=1)
    div = jnp.concatenate(parts[2:], axis=1)
    dtau = jnp.concatenate([dtau_ref[k, pl.ds(j, 1), :] for k in range(2)], axis=1)
    mask = jnp.concatenate([mask_ref[k, pl.ds(j, 1), :] for k in range(2)], axis=1)
    matrix = matrix_ref[...]

    def times(x):
        return jnp.dot(matrix, x, precision=lax.Precision.HIGH, preferred_element_type=jnp.float32)

    new = state - dtau * (div + times(state))
    new = jnp.where(mask > 0, new, state)
    coupled = times(new)
    lanes = dtau_ref.shape[2]
    for q, value in enumerate((new[:, :lanes], new[:, lanes:], coupled[:, :lanes], coupled[:, lanes:])):
        out_ref[pl.ds(q, count, stride=4), :] = value


def call(kernel, shapes, args, scratch_shapes=(), flops=0, aliases=None, keep=True):
    vmem = pl.BlockSpec(memory_space=pltpu.VMEM)
    specs = [pl.BlockSpec(memory_space=pltpu.SMEM)] + [vmem] * (len(args) - 1)
    args = [args[0]] + [pltpu.with_memory_space_constraint(a, pltpu.VMEM) for a in args[1:]]
    held = pltpu.VMEM if keep else jax.ShapeDtypeStruct
    outs = pl.pallas_call(
        kernel,
        out_shape=[held(shape, jnp.float32) for shape in shapes],
        in_specs=specs,
        out_specs=[vmem] * len(shapes),
        scratch_shapes=list(scratch_shapes),
        input_output_aliases=aliases or {},
        cost_estimate=pl.CostEstimate(flops=flops, bytes_accessed=10**6, transcendentals=0),
        compiler_params=pltpu.CompilerParams(vmem_limit_bytes=24 * 2**20),
    )(*args)
    return outs if len(shapes) > 1 else outs[0]


def first_call(place, chunk, field, mask, link, speed, matrix, dtau):
    vmem = pl.BlockSpec(memory_space=pltpu.VMEM)
    nj, ni = mask.shape[1:]
    given = (field, mask, link, speed, matrix, dtau)
    sources = [pltpu.with_memory_space_constraint(a, pltpu.HBM) for a in given]
    outs = [pltpu.VMEM(a.shape, a.dtype) for a in given]
    outs += [pltpu.VMEM(shape, jnp.float32) for shape in (field.shape, (LIVE, nj, ni))]
    return pl.pallas_call(
        first_kernel,
        out_shape=outs,
        in_specs=[pl.BlockSpec(memory_space=pltpu.SMEM)] * 2 + [pl.BlockSpec(memory_space=pltpu.HBM)] * 6,
        out_specs=[vmem] * 8,
        scratch_shapes=[*scratch(nj, ni), pltpu.SemaphoreType.DMA((6,))],
        cost_estimate=pl.CostEstimate(flops=10**8, bytes_accessed=10**6, transcendentals=0),
        compiler_params=pltpu.CompilerParams(vmem_limit_bytes=24 * 2**20),
    )(place, chunk, *sources)


def shards(matrix, state, frame_velocity, dtau, live_mask, link):
    nj, ni = live_mask.shape[1:]
    flaps, gusts = lax.axis_size("flap"), lax.axis_size("gust")
    count = flaps * gusts
    field = state[0, 0]
    first = jnp.where(lax.axis_index("span") == 0, 1, 0).astype(jnp.int32)[None]
    chunk = (lax.axis_index("flap") * gusts + lax.axis_index("gust")).astype(jnp.int32)[None]
    swap = [(0, 1), (1, 0)]

    def turn(x):
        y = lax.all_to_all(x.reshape(count, 4, ni), ("flap", "gust"), 0, 0, tiled=True)
        return y.reshape(count * 4, ni)

    with jax.named_scope("halo"):
        other = lax.ppermute(field, "span", swap)
    with jax.named_scope("first_divergence"):
        held, mask, link, speed, matrix, dtau, div, near = first_call(
            first, chunk, field, live_mask, link[None], frame_velocity[0], matrix, dtau
        )
        pack = call(first_edge_kernel, [(count * 4, ni)], (first, speed, near, other, held, div))
    with jax.named_scope("turn"):
        pack = turn(pack)
    with jax.named_scope("instances"):
        pack = call(instances_kernel, [pack.shape], (chunk, matrix, pack, dtau, mask), (), 10**8)
    with jax.named_scope("turn_back"):
        pack = turn(pack)
    with jax.named_scope("halo"):
        other = lax.ppermute(call(edge_kernel, [(5, nj, ni)], (first, pack)), "span", swap)
    with jax.named_scope("last_divergence"):
        most, near = call(
            last_kernel,
            [field.shape, (LIVE, nj, ni)],
            (first, speed, pack, mask, dtau, link),
            scratch(nj, ni),
            10**8,
        )
        out = call(last_edge_kernel, [field.shape], (first, speed, near, other, most, mask, dtau), keep=False)
    return out[None, None]


def solution(mesh):
    flap = instance_matrix(mesh.shape["flap"], FLAP_OMEGA)
    gust = instance_matrix(mesh.shape["gust"], GUST_OMEGA)
    matrix = np.kron(flap, np.eye(len(gust))) + np.kron(np.eye(len(flap)), gust)
    matrix = jnp.asarray(matrix.astype(np.float32))
    in_specs = (
        P("flap", "gust", None, "span", None, None),
        P("flap", "gust", None),
        P("span", None, None),
        P("span", None, None),
        P(),
    )
    out_specs = P("flap", "gust", None, "span", None, None)
    return jax.shard_map(
        functools.partial(shards, matrix), mesh=mesh, in_specs=in_specs, out_specs=out_specs, check_vma=False
    )
```

```python
import functools
import math

import jax
import jax.numpy as jnp
import numpy as np
from jax import lax
from jax.experimental import pallas as pl
from jax.experimental.pallas import tpu as pltpu
from jax.sharding import PartitionSpec as P

VISC = 0.12
FLAP_OMEGA = 0.8
GUST_OMEGA = 1.2944
HEAD_FLAP, HEAD_GUST = 4, 10

RHO, U, V, W, PR, EN, RT, LIVE = range(8)
PAD = 8


def instance_matrix(count, omega):
    offset = np.arange(count)[:, None] - np.arange(count)[None, :]
    angle = np.pi * offset / count
    parity = np.where(offset % 2 == 0, 1.0, -1.0)
    off = offset != 0
    safe = np.where(off, angle, 0.5 * np.pi)
    first = np.where(off, 0.5 * parity / np.tan(safe), 0.0)
    second = np.where(off, -0.5 * parity / np.sin(safe) ** 2, -(count * count / 12.0 + 1.0 / 6.0))
    return omega * first - VISC * second


def primitives(rho, m1, m2, m3, energy):
    inv = 1.0 / rho
    u, v, w = m1 * inv, m2 * inv, m3 * inv
    p = 0.4 * (energy - 0.5 * (m1 * u + m2 * v + m3 * w))
    return (rho, u, v, w, p, (energy + p) * inv, jnp.sqrt(jnp.abs(rho)))


def physical(cell, axis, g):
    rho, vel, p, enth = 2.0 * cell[RHO], cell[U : W + 1], 2.0 * cell[PR], cell[EN]
    mass = rho * (vel[axis] - g)
    mom = [mass * vel[a] + p if a == axis else mass * vel[a] for a in range(3)]
    return [mass, *mom, mass * enth + g * p]


def roe(left, right, axis, g):
    rho_l, vel_l, p_l, h_l, s_l = left[RHO], left[U : W + 1], left[PR], left[EN], left[RT]
    rho_r, vel_r, p_r, h_r, s_r = right[RHO], right[U : W + 1], right[PR], right[EN], right[RT]
    t1, t2 = [a for a in range(3) if a != axis]
    weight = s_r / (s_l + s_r)
    jump = [vel_r[a] - vel_l[a] for a in range(3)]
    vel = [vel_l[a] + weight * jump[a] for a in range(3)]
    enth = h_l + weight * (h_r - h_l)
    half_sq = 0.5 * (vel[0] * vel[0] + vel[1] * vel[1] + vel[2] * vel[2])
    c_sq = 0.4 * (enth - half_sq)
    inv_c = lax.rsqrt(c_sq)
    c = c_sq * inv_c
    delta = 0.1 * c
    scale = 5.0 * inv_c
    half_inv_sq = 0.5 * (inv_c * inv_c)
    rho_t = s_l * s_r
    dp = p_r - p_l
    drho = rho_r - rho_l
    swing = rho_t * c * jump[axis]

    def speed(value):
        size = jnp.abs(value)
        return jnp.where(size < delta, (value * value + delta * delta) * scale, size)

    rel = vel[axis] - g
    l2 = speed(rel)
    w1 = speed(rel - c) * ((dp - swing) * half_inv_sq)
    w3 = speed(rel + c) * ((dp + swing) * half_inv_sq)
    w2 = l2 * (drho - dp * (2.0 * half_inv_sq))
    shear = l2 * rho_t
    acoustic = w1 + w3
    total = acoustic + w2
    skew = (w3 - w1) * c
    mass_l = rho_l * (vel_l[axis] - g)
    mass_r = rho_r * (vel_r[axis] - g)
    out = [mass_l + mass_r - total]
    for a in range(3):
        flux = mass_l * vel_l[a] + mass_r * vel_r[a]
        if a == axis:
            flux = flux + (p_l + p_r) - (total * vel[a] + skew)
        else:
            flux = flux - (total * vel[a] + shear * jump[a])
        out.append(flux)
    loss = acoustic * enth + w2 * half_sq + skew * vel[axis]
    loss = loss + shear * (vel[t1] * jump[t1] + vel[t2] * jump[t2])
    out.append(mass_l * h_l + mass_r * h_r + g * (p_l + p_r) - loss)
    return out


def walled(left, right, axis):
    live_l, live_r = left[LIVE] > 0.0, right[LIVE] > 0.0
    n = U + axis
    new_l, new_r = [], []
    for f in range(LIVE):
        if f == n:
            new_l.append(jnp.where(live_l, left[f], -right[f]))
            new_r.append(jnp.where(live_r, right[f], -left[f]))
        else:
            new_l.append(jnp.where(live_l, left[f], right[f]))
            new_r.append(jnp.where(live_r, right[f], left[f]))
    return new_l, new_r


def frame(speed_ref, axis):
    return jnp.broadcast_to(speed_ref[:, axis : axis + 1], (8, 128))


def most_of_divergence(load, mask_ref, link_ref, speed_ref, first, cells, faces, emit):
    nj = mask_ref.shape[1]
    blocks = nj // 8
    g0, g1, g2 = [frame(speed_ref, axis) for axis in range(3)]

    def rows(b):
        return pl.multiple_of(8 * b, 8)

    def fill(b, carry):
        row = rows(b)
        for k in range(2):
            values = primitives(*[load(f, k, row) for f in range(5)])
            for f, value in enumerate(values):
                cells[f, k, pl.ds(PAD + row, 8), :] = value
            live = jnp.where(mask_ref[k, pl.ds(row, 8), :] > 0, 1.0, 0.0)
            cells[LIVE, k, pl.ds(PAD + row, 8), :] = live
        return carry

    lax.fori_loop(0, blocks, fill, 0, unroll=True)
    link = jnp.broadcast_to(link_ref[...], (8, link_ref.shape[1]))
    for k in range(2):
        for f in range(8):
            top = cells[f, k, pl.ds(PAD, 8), :]
            below = jnp.take_along_axis(top, link, axis=1)[:1]
            cells[f, k, pl.ds(PAD - 1, 1), :] = below
            last = cells[f, k, pl.ds(PAD + nj - 1, 1), :]
            if f == LIVE:
                last = jnp.ones_like(last)
            cells[f, k, pl.ds(PAD + nj, 8), :] = jnp.broadcast_to(last, (8, last.shape[1]))

    def normal(b, carry):
        row = rows(b)
        for k in range(2):
            left = [cells[f, k, pl.ds(PAD - 1 + row, 8), :] for f in range(8)]
            right = [cells[f, k, pl.ds(PAD + row, 8), :] for f in range(8)]
            flux = roe(*walled(left, right, 1), 1, g1)
            for f in range(5):
                faces[f, k, pl.ds(row, 8), :] = flux[f]
        return carry

    lax.fori_loop(0, blocks + 1, normal, 0, unroll=True)

    def rest(b, carry):
        row = rows(b)
        near = [[cells[f, k, pl.ds(PAD + row, 8), :] for f in range(8)] for k in range(2)]
        inner = roe(near[0], near[1], 2, g2)
        edge = physical([jnp.where(first, near[0][f], near[1][f]) for f in range(7)], 2, g2)
        for k in range(2):
            here = near[k]
            lanes = here[0].shape[1]
            ahead = [pltpu.roll(x, lanes - 1, 1) for x in here]
            chord = roe(*walled(here, ahead, 0), 0, g0)
            for f in range(5):
                after = faces[f, k, pl.ds(row + 1, 8), :] - faces[f, k, pl.ds(row, 8), :]
                after = after + (chord[f] - pltpu.roll(chord[f], 1, 1))
                if k == 0:
                    span = inner[f] - jnp.where(first, edge[f], 0.0)
                else:
                    span = jnp.where(first, 0.0, edge[f]) - inner[f]
                emit(f, k, row, 0.5 * (span + after))
        return carry

    lax.fori_loop(0, blocks, rest, 0, unroll=True)


def outer_face(mine, other, speed_ref, first):
    other = primitives(*other)
    left = [jnp.where(first, a, b) for a, b in zip(mine, other)]
    right = [jnp.where(first, b, a) for a, b in zip(mine, other)]
    sign = jnp.where(first, 0.5, -0.5)
    return [sign * x for x in roe(left, right, 2, frame(speed_ref, 2))]


def scratch(nj, ni):
    return [
        pltpu.VMEM((8, 2, nj + 2 * PAD, ni), jnp.float32),
        pltpu.VMEM((5, 2, nj + PAD, ni), jnp.float32),
    ]


def packed(f, row, q, nj):
    return pl.ds(4 * (f * nj + row) + q, 8, stride=4)


def first_kernel(place_ref, chunk_ref, *refs):
    sources, targets, (out_ref, near_ref, cells, faces, sems) = refs[:6], refs[6:12], refs[12:]
    state_ref, mask_ref, link_ref, speed_ref = targets[:4]
    nj = mask_ref.shape[1]
    copies = [
        pltpu.make_async_copy(source, target, sems.at[i])
        for i, (source, target) in enumerate(zip(sources, targets))
    ]
    for copy in copies:
        copy.start()
    for copy in copies[:4]:
        copy.wait()

    def load(f, k, row):
        return state_ref[f, k, pl.ds(row, 8), :]

    def emit(f, k, row, div):
        out_ref[f, k, pl.ds(row, 8), :] = div

    most_of_divergence(load, mask_ref, link_ref, speed_ref, place_ref[0] > 0, cells, faces, emit)
    near_ref[...] = cells[:LIVE, place_ref[0], PAD : PAD + nj, :]
    for copy in copies[4:]:
        copy.wait()


def first_edge_kernel(place_ref, speed_ref, near_ref, other_ref, state_ref, div_ref, out_ref):
    nj = other_ref.shape[2]
    edge = place_ref[0]
    used = 4 * 5 * nj
    if out_ref.shape[0] > used:
        out_ref[used:, :] = jnp.zeros((out_ref.shape[0] - used, out_ref.shape[1]), jnp.float32)
    for row in range(0, nj, 8):
        block = pl.ds(row, 8)
        mine = [near_ref[f, block, :] for f in range(LIVE)]
        other = [other_ref[f, 1 - edge, block, :] for f in range(5)]
        flux = outer_face(mine, other, speed_ref, edge > 0)
        for f in range(5):
            for k in range(2):
                out_ref[packed(f, row, k, nj), :] = state_ref[f, k, block, :]
            out_ref[packed(f, row, 2 + edge, nj), :] = div_ref[f, edge, block, :] + flux[f]
            out_ref[packed(f, row, 3 - edge, nj), :] = div_ref[f, 1 - edge, block, :]


def last_kernel(place_ref, speed_ref, turned_ref, mask_ref, dtau_ref, link_ref, out_ref, near_ref, cells, faces):
    nj = mask_ref.shape[1]

    def load(f, k, row):
        return turned_ref[packed(f, row, k, nj), :]

    def emit(f, k, row, div):
        block = pl.ds(row, 8)
        old = load(f, k, row)
        new = old - dtau_ref[k, block, :] * (div + turned_ref[packed(f, row, 2 + k, nj), :])
        out_ref[f, k, block, :] = jnp.where(mask_ref[k, block, :] > 0, new, old)

    most_of_divergence(load, mask_ref, link_ref, speed_ref, place_ref[0] > 0, cells, faces, emit)
    near_ref[...] = cells[:LIVE, place_ref[0], PAD : PAD + nj, :]


def last_edge_kernel(place_ref, speed_ref, near_ref, other_ref, most_ref, mask_ref, dtau_ref, out_ref):
    nj = mask_ref.shape[1]
    edge = place_ref[0]
    for f in range(5):
        out_ref[f, 1 - edge, :, :] = most_ref[f, 1 - edge, :, :]
    for row in range(0, nj, 8):
        block = pl.ds(row, 8)
        mine = [near_ref[f, block, :] for f in range(LIVE)]
        flux = outer_face(mine, [other_ref[f, block, :] for f in range(5)], speed_ref, edge > 0)
        live = mask_ref[edge, block, :] > 0
        dtau = dtau_ref[edge, block, :]
        for f in range(5):
            most = most_ref[f, edge, block, :]
            out_ref[f, edge, block, :] = jnp.where(live, most - dtau * flux[f], most)


def edge_kernel(place_ref, turned_ref, out_ref):
    nj = out_ref.shape[1]
    for f in range(5):
        for row in range(0, nj, 8):
            out_ref[f, pl.ds(row, 8), :] = turned_ref[packed(f, row, place_ref[0], nj), :]


def instances_kernel(chunk_ref, matrix_ref, turned_ref, dtau_ref, mask_ref, out_ref):
    count = matrix_ref.shape[0]
    nj = mask_ref.shape[1]
    j = lax.rem(chunk_ref[0], nj)
    parts = [turned_ref[pl.ds(q, count, stride=4), :] for q in range(4)]
    state = jnp.concatenate(parts[:2], axis=1)
    div = jnp.concatenate(parts[2:], axis=1)
    dtau = jnp.concatenate([dtau_ref[k, pl.ds(j, 1), :] for k in range(2)], axis=1)
    mask = jnp.concatenate([mask_ref[k, pl.ds(j, 1), :] for k in range(2)], axis=1)
    matrix = matrix_ref[...]

    def times(x):
        return jnp.dot(matrix, x, precision=lax.Precision.HIGH, preferred_element_type=jnp.float32)

    new = state - dtau * (div + times(state))
    new = jnp.where(mask > 0, new, state)
    coupled = times(new)
    lanes = dtau_ref.shape[2]
    for q, value in enumerate((new[:, :lanes], new[:, lanes:], coupled[:, :lanes], coupled[:, lanes:])):
        out_ref[pl.ds(q, count, stride=4), :] = value


def call(kernel, shapes, args, scratch_shapes=(), flops=0, aliases=None, keep=True):
    vmem = pl.BlockSpec(memory_space=pltpu.VMEM)
    specs = [pl.BlockSpec(memory_space=pltpu.SMEM)] + [vmem] * (len(args) - 1)
    args = [args[0]] + [pltpu.with_memory_space_constraint(a, pltpu.VMEM) for a in args[1:]]
    held = pltpu.VMEM if keep else jax.ShapeDtypeStruct
    outs = pl.pallas_call(
        kernel,
        out_shape=[held(shape, jnp.float32) for shape in shapes],
        in_specs=specs,
        out_specs=[vmem] * len(shapes),
        scratch_shapes=list(scratch_shapes),
        input_output_aliases=aliases or {},
        cost_estimate=pl.CostEstimate(flops=flops, bytes_accessed=10**6, transcendentals=0),
        compiler_params=pltpu.CompilerParams(vmem_limit_bytes=24 * 2**20),
    )(*args)
    return outs if len(shapes) > 1 else outs[0]


def first_call(place, chunk, field, mask, link, speed, matrix, dtau):
    vmem = pl.BlockSpec(memory_space=pltpu.VMEM)
    nj, ni = mask.shape[1:]
    given = (field, mask, link, speed, matrix, dtau)
    sources = [pltpu.with_memory_space_constraint(a, pltpu.HBM) for a in given]
    outs = [pltpu.VMEM(a.shape, a.dtype) for a in given]
    outs += [pltpu.VMEM(shape, jnp.float32) for shape in (field.shape, (LIVE, nj, ni))]
    return pl.pallas_call(
        first_kernel,
        out_shape=outs,
        in_specs=[pl.BlockSpec(memory_space=pltpu.SMEM)] * 2 + [pl.BlockSpec(memory_space=pltpu.HBM)] * 6,
        out_specs=[vmem] * 8,
        scratch_shapes=[*scratch(nj, ni), pltpu.SemaphoreType.DMA((6,))],
        cost_estimate=pl.CostEstimate(flops=10**8, bytes_accessed=10**6, transcendentals=0),
        compiler_params=pltpu.CompilerParams(vmem_limit_bytes=24 * 2**20),
    )(place, chunk, *sources)


def shards(head, matrix, state, frame_velocity, dtau, live_mask, link):
    nj, ni = live_mask.shape[1:]
    flaps, gusts = lax.axis_size("flap"), lax.axis_size("gust")
    count = flaps * gusts
    field = state[0, 0]
    first = jnp.where(lax.axis_index("span") == 0, 1, 0).astype(jnp.int32)[None]
    chunk = lax.axis_index("flap") * gusts + lax.axis_index("gust")
    chunk = jnp.where(chunk == 0, head, jnp.where(chunk == head, 0, chunk)).astype(jnp.int32)[None]
    order = headed(count, head)
    swap = [(0, 1), (1, 0)]

    def turn(x):
        y = lax.all_to_all(x.reshape(count, 4, ni), ("flap", "gust"), 0, 0, tiled=True, axis_index_groups=[order])
        return y.reshape(count * 4, ni)

    with jax.named_scope("halo"):
        other = lax.ppermute(field, "span", swap)
    with jax.named_scope("first_divergence"):
        held, mask, link, speed, matrix, dtau, div, near = first_call(
            first, chunk, field, live_mask, link[None], frame_velocity[0], matrix, dtau
        )
        pack = call(first_edge_kernel, [(count * 4, ni)], (first, speed, near, other, held, div))
    with jax.named_scope("turn"):
        pack = turn(pack)
    with jax.named_scope("instances"):
        pack = call(instances_kernel, [pack.shape], (chunk, matrix, pack, dtau, mask), (), 10**8)
    with jax.named_scope("turn_back"):
        pack = turn(pack)
    with jax.named_scope("halo"):
        other = lax.ppermute(call(edge_kernel, [(5, nj, ni)], (first, pack)), "span", swap)
    with jax.named_scope("last_divergence"):
        most, near = call(
            last_kernel,
            [field.shape, (LIVE, nj, ni)],
            (first, speed, pack, mask, dtau, link),
            scratch(nj, ni),
            10**8,
        )
        out = call(last_edge_kernel, [field.shape], (first, speed, near, other, most, mask, dtau), keep=False)
    return out[None, None]


def headed(count, head):
    order = list(range(count))
    order[0], order[head] = head, 0
    return order


def solution(mesh):
    flap = instance_matrix(mesh.shape["flap"], FLAP_OMEGA)
    gust = instance_matrix(mesh.shape["gust"], GUST_OMEGA)
    matrix = np.kron(flap, np.eye(len(gust))) + np.kron(np.eye(len(flap)), gust)
    head = HEAD_FLAP * len(gust) + HEAD_GUST
    order = headed(len(matrix), head)
    matrix = jnp.asarray(matrix[order][:, order].astype(np.float32))
    in_specs = (
        P("flap", "gust", None, "span", None, None),
        P("flap", "gust", None),
        P("span", None, None),
        P("span", None, None),
        P(),
    )
    out_specs = P("flap", "gust", None, "span", None, None)
    return jax.shard_map(
        functools.partial(shards, head, matrix), mesh=mesh, in_specs=in_specs, out_specs=out_specs, check_vma=False
    )
```

```python
import functools
import math

import jax
import jax.numpy as jnp
import numpy as np
from jax import lax
from jax.experimental import pallas as pl
from jax.experimental.pallas import tpu as pltpu
from jax.sharding import PartitionSpec as P

VISC = 0.12
FLAP_OMEGA = 0.8
GUST_OMEGA = 1.2944
HEAD_FLAP, HEAD_GUST = 12, 10

RHO, U, V, W, PR, EN, RT, LIVE = range(8)
PAD = 8


def instance_matrix(count, omega):
    offset = np.arange(count)[:, None] - np.arange(count)[None, :]
    angle = np.pi * offset / count
    parity = np.where(offset % 2 == 0, 1.0, -1.0)
    off = offset != 0
    safe = np.where(off, angle, 0.5 * np.pi)
    first = np.where(off, 0.5 * parity / np.tan(safe), 0.0)
    second = np.where(off, -0.5 * parity / np.sin(safe) ** 2, -(count * count / 12.0 + 1.0 / 6.0))
    return omega * first - VISC * second


def primitives(rho, m1, m2, m3, energy):
    inv = 1.0 / rho
    u, v, w = m1 * inv, m2 * inv, m3 * inv
    p = 0.4 * (energy - 0.5 * (m1 * u + m2 * v + m3 * w))
    return (rho, u, v, w, p, (energy + p) * inv, jnp.sqrt(jnp.abs(rho)))


def physical(cell, axis, g):
    rho, vel, p, enth = 2.0 * cell[RHO], cell[U : W + 1], 2.0 * cell[PR], cell[EN]
    mass = rho * (vel[axis] - g)
    mom = [mass * vel[a] + p if a == axis else mass * vel[a] for a in range(3)]
    return [mass, *mom, mass * enth + g * p]


def roe(left, right, axis, g):
    rho_l, vel_l, p_l, h_l, s_l = left[RHO], left[U : W + 1], left[PR], left[EN], left[RT]
    rho_r, vel_r, p_r, h_r, s_r = right[RHO], right[U : W + 1], right[PR], right[EN], right[RT]
    t1, t2 = [a for a in range(3) if a != axis]
    weight = s_r / (s_l + s_r)
    jump = [vel_r[a] - vel_l[a] for a in range(3)]
    vel = [vel_l[a] + weight * jump[a] for a in range(3)]
    enth = h_l + weight * (h_r - h_l)
    half_sq = 0.5 * (vel[0] * vel[0] + vel[1] * vel[1] + vel[2] * vel[2])
    c_sq = 0.4 * (enth - half_sq)
    inv_c = lax.rsqrt(c_sq)
    c = c_sq * inv_c
    delta = 0.1 * c
    scale = 5.0 * inv_c
    half_inv_sq = 0.5 * (inv_c * inv_c)
    rho_t = s_l * s_r
    dp = p_r - p_l
    drho = rho_r - rho_l
    swing = rho_t * c * jump[axis]

    def speed(value):
        size = jnp.abs(value)
        return jnp.where(size < delta, (value * value + delta * delta) * scale, size)

    rel = vel[axis] - g
    l2 = speed(rel)
    w1 = speed(rel - c) * ((dp - swing) * half_inv_sq)
    w3 = speed(rel + c) * ((dp + swing) * half_inv_sq)
    w2 = l2 * (drho - dp * (2.0 * half_inv_sq))
    shear = l2 * rho_t
    acoustic = w1 + w3
    total = acoustic + w2
    skew = (w3 - w1) * c
    mass_l = rho_l * (vel_l[axis] - g)
    mass_r = rho_r * (vel_r[axis] - g)
    out = [mass_l + mass_r - total]
    for a in range(3):
        flux = mass_l * vel_l[a] + mass_r * vel_r[a]
        if a == axis:
            flux = flux + (p_l + p_r) - (total * vel[a] + skew)
        else:
            flux = flux - (total * vel[a] + shear * jump[a])
        out.append(flux)
    loss = acoustic * enth + w2 * half_sq + skew * vel[axis]
    loss = loss + shear * (vel[t1] * jump[t1] + vel[t2] * jump[t2])
    out.append(mass_l * h_l + mass_r * h_r + g * (p_l + p_r) - loss)
    return out


def walled(left, right, axis):
    live_l, live_r = left[LIVE] > 0.0, right[LIVE] > 0.0
    n = U + axis
    new_l, new_r = [], []
    for f in range(LIVE):
        if f == n:
            new_l.append(jnp.where(live_l, left[f], -right[f]))
            new_r.append(jnp.where(live_r, right[f], -left[f]))
        else:
            new_l.append(jnp.where(live_l, left[f], right[f]))
            new_r.append(jnp.where(live_r, right[f], left[f]))
    return new_l, new_r


def frame(speed_ref, axis):
    return jnp.broadcast_to(speed_ref[:, axis : axis + 1], (8, 128))


def most_of_divergence(load, mask_ref, link_ref, speed_ref, first, cells, faces, emit):
    nj = mask_ref.shape[1]
    blocks = nj // 8
    g0, g1, g2 = [frame(speed_ref, axis) for axis in range(3)]

    def rows(b):
        return pl.multiple_of(8 * b, 8)

    def fill(b, carry):
        row = rows(b)
        for k in range(2):
            values = primitives(*[load(f, k, row) for f in range(5)])
            for f, value in enumerate(values):
                cells[f, k, pl.ds(PAD + row, 8), :] = value
            live = jnp.where(mask_ref[k, pl.ds(row, 8), :] > 0, 1.0, 0.0)
            cells[LIVE, k, pl.ds(PAD + row, 8), :] = live
        return carry

    lax.fori_loop(0, blocks, fill, 0, unroll=True)
    link = jnp.broadcast_to(link_ref[...], (8, link_ref.shape[1]))
    for k in range(2):
        for f in range(8):
            top = cells[f, k, pl.ds(PAD, 8), :]
            below = jnp.take_along_axis(top, link, axis=1)[:1]
            cells[f, k, pl.ds(PAD - 1, 1), :] = below
            last = cells[f, k, pl.ds(PAD + nj - 1, 1), :]
            if f == LIVE:
                last = jnp.ones_like(last)
            cells[f, k, pl.ds(PAD + nj, 8), :] = jnp.broadcast_to(last, (8, last.shape[1]))

    def normal(b, carry):
        row = rows(b)
        for k in range(2):
            left = [cells[f, k, pl.ds(PAD - 1 + row, 8), :] for f in range(8)]
            right = [cells[f, k, pl.ds(PAD + row, 8), :] for f in range(8)]
            flux = roe(*walled(left, right, 1), 1, g1)
            for f in range(5):
                faces[f, k, pl.ds(row, 8), :] = flux[f]
        return carry

    lax.fori_loop(0, blocks + 1, normal, 0, unroll=True)

    def rest(b, carry):
        row = rows(b)
        near = [[cells[f, k, pl.ds(PAD + row, 8), :] for f in range(8)] for k in range(2)]
        inner = roe(near[0], near[1], 2, g2)
        edge = physical([jnp.where(first, near[0][f], near[1][f]) for f in range(7)], 2, g2)
        for k in range(2):
            here = near[k]
            lanes = here[0].shape[1]
            ahead = [pltpu.roll(x, lanes - 1, 1) for x in here]
            chord = roe(*walled(here, ahead, 0), 0, g0)
            for f in range(5):
                after = faces[f, k, pl.ds(row + 1, 8), :] - faces[f, k, pl.ds(row, 8), :]
                after = after + (chord[f] - pltpu.roll(chord[f], 1, 1))
                if k == 0:
                    span = inner[f] - jnp.where(first, edge[f], 0.0)
                else:
                    span = jnp.where(first, 0.0, edge[f]) - inner[f]
                emit(f, k, row, 0.5 * (span + after))
        return carry

    lax.fori_loop(0, blocks, rest, 0, unroll=True)


def outer_face(mine, other, speed_ref, first):
    other = primitives(*other)
    left = [jnp.where(first, a, b) for a, b in zip(mine, other)]
    right = [jnp.where(first, b, a) for a, b in zip(mine, other)]
    sign = jnp.where(first, 0.5, -0.5)
    return [sign * x for x in roe(left, right, 2, frame(speed_ref, 2))]


def scratch(nj, ni):
    return [
        pltpu.VMEM((8, 2, nj + 2 * PAD, ni), jnp.float32),
        pltpu.VMEM((5, 2, nj + PAD, ni), jnp.float32),
    ]


def packed(f, row, q, nj):
    return pl.ds(4 * (f * nj + row) + q, 8, stride=4)


def first_kernel(place_ref, chunk_ref, *refs):
    sources, targets, (out_ref, near_ref, cells, faces, sems) = refs[:6], refs[6:12], refs[12:]
    state_ref, mask_ref, link_ref, speed_ref = targets[:4]
    nj = mask_ref.shape[1]
    copies = [
        pltpu.make_async_copy(source, target, sems.at[i])
        for i, (source, target) in enumerate(zip(sources, targets))
    ]
    for copy in copies:
        copy.start()
    for copy in copies[:4]:
        copy.wait()

    def load(f, k, row):
        return state_ref[f, k, pl.ds(row, 8), :]

    def emit(f, k, row, div):
        out_ref[f, k, pl.ds(row, 8), :] = div

    most_of_divergence(load, mask_ref, link_ref, speed_ref, place_ref[0] > 0, cells, faces, emit)
    near_ref[...] = cells[:LIVE, place_ref[0], PAD : PAD + nj, :]
    for copy in copies[4:]:
        copy.wait()


def first_edge_kernel(place_ref, speed_ref, near_ref, other_ref, state_ref, div_ref, out_ref):
    nj = other_ref.shape[2]
    edge = place_ref[0]
    used = 4 * 5 * nj
    if out_ref.shape[0] > used:
        out_ref[used:, :] = jnp.zeros((out_ref.shape[0] - used, out_ref.shape[1]), jnp.float32)
    for row in range(0, nj, 8):
        block = pl.ds(row, 8)
        mine = [near_ref[f, block, :] for f in range(LIVE)]
        other = [other_ref[f, 1 - edge, block, :] for f in range(5)]
        flux = outer_face(mine, other, speed_ref, edge > 0)
        for f in range(5):
            for k in range(2):
                out_ref[packed(f, row, k, nj), :] = state_ref[f, k, block, :]
            out_ref[packed(f, row, 2 + edge, nj), :] = div_ref[f, edge, block, :] + flux[f]
            out_ref[packed(f, row, 3 - edge, nj), :] = div_ref[f, 1 - edge, block, :]


def last_kernel(place_ref, speed_ref, turned_ref, mask_ref, dtau_ref, link_ref, out_ref, near_ref, cells, faces):
    nj = mask_ref.shape[1]

    def load(f, k, row):
        return turned_ref[packed(f, row, k, nj), :]

    def emit(f, k, row, div):
        block = pl.ds(row, 8)
        old = load(f, k, row)
        new = old - dtau_ref[k, block, :] * (div + turned_ref[packed(f, row, 2 + k, nj), :])
        out_ref[f, k, block, :] = jnp.where(mask_ref[k, block, :] > 0, new, old)

    most_of_divergence(load, mask_ref, link_ref, speed_ref, place_ref[0] > 0, cells, faces, emit)
    near_ref[...] = cells[:LIVE, place_ref[0], PAD : PAD + nj, :]


def last_edge_kernel(place_ref, speed_ref, near_ref, other_ref, most_ref, mask_ref, dtau_ref, out_ref):
    nj = mask_ref.shape[1]
    edge = place_ref[0]
    for f in range(5):
        out_ref[f, 1 - edge, :, :] = most_ref[f, 1 - edge, :, :]
    for row in range(0, nj, 8):
        block = pl.ds(row, 8)
        mine = [near_ref[f, block, :] for f in range(LIVE)]
        flux = outer_face(mine, [other_ref[f, block, :] for f in range(5)], speed_ref, edge > 0)
        live = mask_ref[edge, block, :] > 0
        dtau = dtau_ref[edge, block, :]
        for f in range(5):
            most = most_ref[f, edge, block, :]
            out_ref[f, edge, block, :] = jnp.where(live, most - dtau * flux[f], most)


def edge_kernel(place_ref, turned_ref, out_ref):
    nj = out_ref.shape[1]
    for f in range(5):
        for row in range(0, nj, 8):
            out_ref[f, pl.ds(row, 8), :] = turned_ref[packed(f, row, place_ref[0], nj), :]


def instances_kernel(chunk_ref, matrix_ref, turned_ref, dtau_ref, mask_ref, out_ref):
    count = matrix_ref.shape[0]
    nj = mask_ref.shape[1]
    j = lax.rem(chunk_ref[0], nj)
    parts = [turned_ref[pl.ds(q, count, stride=4), :] for q in range(4)]
    state = jnp.concatenate(parts[:2], axis=1)
    div = jnp.concatenate(parts[2:], axis=1)
    dtau = jnp.concatenate([dtau_ref[k, pl.ds(j, 1), :] for k in range(2)], axis=1)
    mask = jnp.concatenate([mask_ref[k, pl.ds(j, 1), :] for k in range(2)], axis=1)
    matrix = matrix_ref[...]

    def times(x):
        return jnp.dot(matrix, x, precision=lax.Precision.HIGH, preferred_element_type=jnp.float32)

    new = state - dtau * (div + times(state))
    new = jnp.where(mask > 0, new, state)
    coupled = times(new)
    lanes = dtau_ref.shape[2]
    for q, value in enumerate((new[:, :lanes], new[:, lanes:], coupled[:, :lanes], coupled[:, lanes:])):
        out_ref[pl.ds(q, count, stride=4), :] = value


def call(kernel, shapes, args, scratch_shapes=(), flops=0, aliases=None, keep=True):
    vmem = pl.BlockSpec(memory_space=pltpu.VMEM)
    specs = [pl.BlockSpec(memory_space=pltpu.SMEM)] + [vmem] * (len(args) - 1)
    args = [args[0]] + [pltpu.with_memory_space_constraint(a, pltpu.VMEM) for a in args[1:]]
    held = pltpu.VMEM if keep else jax.ShapeDtypeStruct
    outs = pl.pallas_call(
        kernel,
        out_shape=[held(shape, jnp.float32) for shape in shapes],
        in_specs=specs,
        out_specs=[vmem] * len(shapes),
        scratch_shapes=list(scratch_shapes),
        input_output_aliases=aliases or {},
        cost_estimate=pl.CostEstimate(flops=flops, bytes_accessed=10**6, transcendentals=0),
        compiler_params=pltpu.CompilerParams(vmem_limit_bytes=24 * 2**20),
    )(*args)
    return outs if len(shapes) > 1 else outs[0]


def first_call(place, chunk, field, mask, link, speed, matrix, dtau):
    vmem = pl.BlockSpec(memory_space=pltpu.VMEM)
    nj, ni = mask.shape[1:]
    given = (field, mask, link, speed, matrix, dtau)
    sources = [pltpu.with_memory_space_constraint(a, pltpu.HBM) for a in given]
    outs = [pltpu.VMEM(a.shape, a.dtype) for a in given]
    outs += [pltpu.VMEM(shape, jnp.float32) for shape in (field.shape, (LIVE, nj, ni))]
    return pl.pallas_call(
        first_kernel,
        out_shape=outs,
        in_specs=[pl.BlockSpec(memory_space=pltpu.SMEM)] * 2 + [pl.BlockSpec(memory_space=pltpu.HBM)] * 6,
        out_specs=[vmem] * 8,
        scratch_shapes=[*scratch(nj, ni), pltpu.SemaphoreType.DMA((6,))],
        cost_estimate=pl.CostEstimate(flops=10**8, bytes_accessed=10**6, transcendentals=0),
        compiler_params=pltpu.CompilerParams(vmem_limit_bytes=24 * 2**20),
    )(place, chunk, *sources)


def shards(head, matrix, state, frame_velocity, dtau, live_mask, link):
    nj, ni = live_mask.shape[1:]
    flaps, gusts = lax.axis_size("flap"), lax.axis_size("gust")
    count = flaps * gusts
    field = state[0, 0]
    first = jnp.where(lax.axis_index("span") == 0, 1, 0).astype(jnp.int32)[None]
    chunk = lax.axis_index("flap") * gusts + lax.axis_index("gust")
    chunk = jnp.where(chunk == 0, head, jnp.where(chunk == head, 0, chunk)).astype(jnp.int32)[None]
    order = headed(count, head)
    swap = [(0, 1), (1, 0)]

    def turn(x):
        y = lax.all_to_all(x.reshape(count, 4, ni), ("flap", "gust"), 0, 0, tiled=True, axis_index_groups=[order])
        return y.reshape(count * 4, ni)

    with jax.named_scope("halo"):
        other = lax.ppermute(field, "span", swap)
    with jax.named_scope("first_divergence"):
        held, mask, link, speed, matrix, dtau, div, near = first_call(
            first, chunk, field, live_mask, link[None], frame_velocity[0], matrix, dtau
        )
        pack = call(first_edge_kernel, [(count * 4, ni)], (first, speed, near, other, held, div))
    with jax.named_scope("turn"):
        pack = turn(pack)
    with jax.named_scope("instances"):
        pack = call(instances_kernel, [pack.shape], (chunk, matrix, pack, dtau, mask), (), 10**8)
    with jax.named_scope("turn_back"):
        pack = turn(pack)
    with jax.named_scope("halo"):
        other = lax.ppermute(call(edge_kernel, [(5, nj, ni)], (first, pack)), "span", swap)
    with jax.named_scope("last_divergence"):
        most, near = call(
            last_kernel,
            [field.shape, (LIVE, nj, ni)],
            (first, speed, pack, mask, dtau, link),
            scratch(nj, ni),
            10**8,
        )
        out = call(last_edge_kernel, [field.shape], (first, speed, near, other, most, mask, dtau), keep=False)
    return out[None, None]


def headed(count, head):
    order = list(range(count))
    order[0], order[head] = head, 0
    return order


def solution(mesh):
    flap = instance_matrix(mesh.shape["flap"], FLAP_OMEGA)
    gust = instance_matrix(mesh.shape["gust"], GUST_OMEGA)
    matrix = np.kron(flap, np.eye(len(gust))) + np.kron(np.eye(len(flap)), gust)
    head = HEAD_FLAP * len(gust) + HEAD_GUST
    order = headed(len(matrix), head)
    matrix = jnp.asarray(matrix[order][:, order].astype(np.float32))
    in_specs = (
        P("flap", "gust", None, "span", None, None),
        P("flap", "gust", None),
        P("span", None, None),
        P("span", None, None),
        P(),
    )
    out_specs = P("flap", "gust", None, "span", None, None)
    return jax.shard_map(
        functools.partial(shards, head, matrix), mesh=mesh, in_specs=in_specs, out_specs=out_specs, check_vma=False
    )
```

```python
import functools
import math

import jax
import jax.numpy as jnp
import numpy as np
from jax import lax
from jax.experimental import pallas as pl
from jax.experimental.pallas import tpu as pltpu
from jax.sharding import PartitionSpec as P

VISC = 0.12
FLAP_OMEGA = 0.8
GUST_OMEGA = 1.2944
HEAD_FLAP, HEAD_GUST = 12, 14

RHO, U, V, W, PR, EN, RT, LIVE = range(8)
PAD = 8


def instance_matrix(count, omega):
    offset = np.arange(count)[:, None] - np.arange(count)[None, :]
    angle = np.pi * offset / count
    parity = np.where(offset % 2 == 0, 1.0, -1.0)
    off = offset != 0
    safe = np.where(off, angle, 0.5 * np.pi)
    first = np.where(off, 0.5 * parity / np.tan(safe), 0.0)
    second = np.where(off, -0.5 * parity / np.sin(safe) ** 2, -(count * count / 12.0 + 1.0 / 6.0))
    return omega * first - VISC * second


def primitives(rho, m1, m2, m3, energy):
    inv = 1.0 / rho
    u, v, w = m1 * inv, m2 * inv, m3 * inv
    p = 0.4 * (energy - 0.5 * (m1 * u + m2 * v + m3 * w))
    return (rho, u, v, w, p, (energy + p) * inv, jnp.sqrt(jnp.abs(rho)))


def physical(cell, axis, g):
    rho, vel, p, enth = 2.0 * cell[RHO], cell[U : W + 1], 2.0 * cell[PR], cell[EN]
    mass = rho * (vel[axis] - g)
    mom = [mass * vel[a] + p if a == axis else mass * vel[a] for a in range(3)]
    return [mass, *mom, mass * enth + g * p]


def roe(left, right, axis, g):
    rho_l, vel_l, p_l, h_l, s_l = left[RHO], left[U : W + 1], left[PR], left[EN], left[RT]
    rho_r, vel_r, p_r, h_r, s_r = right[RHO], right[U : W + 1], right[PR], right[EN], right[RT]
    t1, t2 = [a for a in range(3) if a != axis]
    weight = s_r / (s_l + s_r)
    jump = [vel_r[a] - vel_l[a] for a in range(3)]
    vel = [vel_l[a] + weight * jump[a] for a in range(3)]
    enth = h_l + weight * (h_r - h_l)
    half_sq = 0.5 * (vel[0] * vel[0] + vel[1] * vel[1] + vel[2] * vel[2])
    c_sq = 0.4 * (enth - half_sq)
    inv_c = lax.rsqrt(c_sq)
    c = c_sq * inv_c
    delta = 0.1 * c
    scale = 5.0 * inv_c
    half_inv_sq = 0.5 * (inv_c * inv_c)
    rho_t = s_l * s_r
    dp = p_r - p_l
    drho = rho_r - rho_l
    swing = rho_t * c * jump[axis]

    def speed(value):
        size = jnp.abs(value)
        return jnp.where(size < delta, (value * value + delta * delta) * scale, size)

    rel = vel[axis] - g
    l2 = speed(rel)
    w1 = speed(rel - c) * ((dp - swing) * half_inv_sq)
    w3 = speed(rel + c) * ((dp + swing) * half_inv_sq)
    w2 = l2 * (drho - dp * (2.0 * half_inv_sq))
    shear = l2 * rho_t
    acoustic = w1 + w3
    total = acoustic + w2
    skew = (w3 - w1) * c
    mass_l = rho_l * (vel_l[axis] - g)
    mass_r = rho_r * (vel_r[axis] - g)
    out = [mass_l + mass_r - total]
    for a in range(3):
        flux = mass_l * vel_l[a] + mass_r * vel_r[a]
        if a == axis:
            flux = flux + (p_l + p_r) - (total * vel[a] + skew)
        else:
            flux = flux - (total * vel[a] + shear * jump[a])
        out.append(flux)
    loss = acoustic * enth + w2 * half_sq + skew * vel[axis]
    loss = loss + shear * (vel[t1] * jump[t1] + vel[t2] * jump[t2])
    out.append(mass_l * h_l + mass_r * h_r + g * (p_l + p_r) - loss)
    return out


def walled(left, right, axis):
    live_l, live_r = left[LIVE] > 0.0, right[LIVE] > 0.0
    n = U + axis
    new_l, new_r = [], []
    for f in range(LIVE):
        if f == n:
            new_l.append(jnp.where(live_l, left[f], -right[f]))
            new_r.append(jnp.where(live_r, right[f], -left[f]))
        else:
            new_l.append(jnp.where(live_l, left[f], right[f]))
            new_r.append(jnp.where(live_r, right[f], left[f]))
    return new_l, new_r


def frame(speed_ref, axis):
    return jnp.broadcast_to(speed_ref[:, axis : axis + 1], (8, 128))


def most_of_divergence(load, mask_ref, link_ref, speed_ref, first, cells, faces, emit):
    nj = mask_ref.shape[1]
    blocks = nj // 8
    g0, g1, g2 = [frame(speed_ref, axis) for axis in range(3)]

    def rows(b):
        return pl.multiple_of(8 * b, 8)

    def fill(b, carry):
        row = rows(b)
        for k in range(2):
            values = primitives(*[load(f, k, row) for f in range(5)])
            for f, value in enumerate(values):
                cells[f, k, pl.ds(PAD + row, 8), :] = value
            live = jnp.where(mask_ref[k, pl.ds(row, 8), :] > 0, 1.0, 0.0)
            cells[LIVE, k, pl.ds(PAD + row, 8), :] = live
        return carry

    lax.fori_loop(0, blocks, fill, 0, unroll=True)
    link = jnp.broadcast_to(link_ref[...], (8, link_ref.shape[1]))
    for k in range(2):
        for f in range(8):
            top = cells[f, k, pl.ds(PAD, 8), :]
            below = jnp.take_along_axis(top, link, axis=1)[:1]
            cells[f, k, pl.ds(PAD - 1, 1), :] = below
            last = cells[f, k, pl.ds(PAD + nj - 1, 1), :]
            if f == LIVE:
                last = jnp.ones_like(last)
            cells[f, k, pl.ds(PAD + nj, 8), :] = jnp.broadcast_to(last, (8, last.shape[1]))

    def normal(b, carry):
        row = rows(b)
        for k in range(2):
            left = [cells[f, k, pl.ds(PAD - 1 + row, 8), :] for f in range(8)]
            right = [cells[f, k, pl.ds(PAD + row, 8), :] for f in range(8)]
            flux = roe(*walled(left, right, 1), 1, g1)
            for f in range(5):
                faces[f, k, pl.ds(row, 8), :] = flux[f]
        return carry

    lax.fori_loop(0, blocks + 1, normal, 0, unroll=True)

    def rest(b, carry):
        row = rows(b)
        near = [[cells[f, k, pl.ds(PAD + row, 8), :] for f in range(8)] for k in range(2)]
        inner = roe(near[0], near[1], 2, g2)
        edge = physical([jnp.where(first, near[0][f], near[1][f]) for f in range(7)], 2, g2)
        for k in range(2):
            here = near[k]
            lanes = here[0].shape[1]
            ahead = [pltpu.roll(x, lanes - 1, 1) for x in here]
            chord = roe(*walled(here, ahead, 0), 0, g0)
            for f in range(5):
                after = faces[f, k, pl.ds(row + 1, 8), :] - faces[f, k, pl.ds(row, 8), :]
                after = after + (chord[f] - pltpu.roll(chord[f], 1, 1))
                if k == 0:
                    span = inner[f] - jnp.where(first, edge[f], 0.0)
                else:
                    span = jnp.where(first, 0.0, edge[f]) - inner[f]
                emit(f, k, row, 0.5 * (span + after))
        return carry

    lax.fori_loop(0, blocks, rest, 0, unroll=True)


def outer_face(mine, other, speed_ref, first):
    other = primitives(*other)
    left = [jnp.where(first, a, b) for a, b in zip(mine, other)]
    right = [jnp.where(first, b, a) for a, b in zip(mine, other)]
    sign = jnp.where(first, 0.5, -0.5)
    return [sign * x for x in roe(left, right, 2, frame(speed_ref, 2))]


def scratch(nj, ni):
    return [
        pltpu.VMEM((8, 2, nj + 2 * PAD, ni), jnp.float32),
        pltpu.VMEM((5, 2, nj + PAD, ni), jnp.float32),
    ]


def packed(f, row, q, nj):
    return pl.ds(4 * (f * nj + row) + q, 8, stride=4)


def first_kernel(place_ref, chunk_ref, *refs):
    sources, targets, (out_ref, near_ref, cells, faces, sems) = refs[:6], refs[6:12], refs[12:]
    state_ref, mask_ref, link_ref, speed_ref = targets[:4]
    nj = mask_ref.shape[1]
    copies = [
        pltpu.make_async_copy(source, target, sems.at[i])
        for i, (source, target) in enumerate(zip(sources, targets))
    ]
    for copy in copies:
        copy.start()
    for copy in copies[:4]:
        copy.wait()

    def load(f, k, row):
        return state_ref[f, k, pl.ds(row, 8), :]

    def emit(f, k, row, div):
        out_ref[f, k, pl.ds(row, 8), :] = div

    most_of_divergence(load, mask_ref, link_ref, speed_ref, place_ref[0] > 0, cells, faces, emit)
    near_ref[...] = cells[:LIVE, place_ref[0], PAD : PAD + nj, :]
    for copy in copies[4:]:
        copy.wait()


def first_edge_kernel(place_ref, speed_ref, near_ref, other_ref, state_ref, div_ref, out_ref):
    nj = other_ref.shape[2]
    edge = place_ref[0]
    used = 4 * 5 * nj
    if out_ref.shape[0] > used:
        out_ref[used:, :] = jnp.zeros((out_ref.shape[0] - used, out_ref.shape[1]), jnp.float32)
    for row in range(0, nj, 8):
        block = pl.ds(row, 8)
        mine = [near_ref[f, block, :] for f in range(LIVE)]
        other = [other_ref[f, 1 - edge, block, :] for f in range(5)]
        flux = outer_face(mine, other, speed_ref, edge > 0)
        for f in range(5):
            for k in range(2):
                out_ref[packed(f, row, k, nj), :] = state_ref[f, k, block, :]
            out_ref[packed(f, row, 2 + edge, nj), :] = div_ref[f, edge, block, :] + flux[f]
            out_ref[packed(f, row, 3 - edge, nj), :] = div_ref[f, 1 - edge, block, :]


def last_kernel(place_ref, speed_ref, turned_ref, mask_ref, dtau_ref, link_ref, out_ref, near_ref, cells, faces):
    nj = mask_ref.shape[1]

    def load(f, k, row):
        return turned_ref[packed(f, row, k, nj), :]

    def emit(f, k, row, div):
        block = pl.ds(row, 8)
        old = load(f, k, row)
        new = old - dtau_ref[k, block, :] * (div + turned_ref[packed(f, row, 2 + k, nj), :])
        out_ref[f, k, block, :] = jnp.where(mask_ref[k, block, :] > 0, new, old)

    most_of_divergence(load, mask_ref, link_ref, speed_ref, place_ref[0] > 0, cells, faces, emit)
    near_ref[...] = cells[:LIVE, place_ref[0], PAD : PAD + nj, :]


def last_edge_kernel(place_ref, speed_ref, near_ref, other_ref, most_ref, mask_ref, dtau_ref, out_ref):
    nj = mask_ref.shape[1]
    edge = place_ref[0]
    for f in range(5):
        out_ref[f, 1 - edge, :, :] = most_ref[f, 1 - edge, :, :]
    for row in range(0, nj, 8):
        block = pl.ds(row, 8)
        mine = [near_ref[f, block, :] for f in range(LIVE)]
        flux = outer_face(mine, [other_ref[f, block, :] for f in range(5)], speed_ref, edge > 0)
        live = mask_ref[edge, block, :] > 0
        dtau = dtau_ref[edge, block, :]
        for f in range(5):
            most = most_ref[f, edge, block, :]
            out_ref[f, edge, block, :] = jnp.where(live, most - dtau * flux[f], most)


def edge_kernel(place_ref, turned_ref, out_ref):
    nj = out_ref.shape[1]
    for f in range(5):
        for row in range(0, nj, 8):
            out_ref[f, pl.ds(row, 8), :] = turned_ref[packed(f, row, place_ref[0], nj), :]


def instances_kernel(chunk_ref, matrix_ref, turned_ref, dtau_ref, mask_ref, out_ref):
    count = matrix_ref.shape[0]
    nj = mask_ref.shape[1]
    j = lax.rem(chunk_ref[0], nj)
    parts = [turned_ref[pl.ds(q, count, stride=4), :] for q in range(4)]
    state = jnp.concatenate(parts[:2], axis=1)
    div = jnp.concatenate(parts[2:], axis=1)
    dtau = jnp.concatenate([dtau_ref[k, pl.ds(j, 1), :] for k in range(2)], axis=1)
    mask = jnp.concatenate([mask_ref[k, pl.ds(j, 1), :] for k in range(2)], axis=1)
    matrix = matrix_ref[...]

    def times(x):
        return jnp.dot(matrix, x, precision=lax.Precision.HIGH, preferred_element_type=jnp.float32)

    new = state - dtau * (div + times(state))
    new = jnp.where(mask > 0, new, state)
    coupled = times(new)
    lanes = dtau_ref.shape[2]
    for q, value in enumerate((new[:, :lanes], new[:, lanes:], coupled[:, :lanes], coupled[:, lanes:])):
        out_ref[pl.ds(q, count, stride=4), :] = value


def call(kernel, shapes, args, scratch_shapes=(), flops=0, aliases=None, keep=True):
    vmem = pl.BlockSpec(memory_space=pltpu.VMEM)
    specs = [pl.BlockSpec(memory_space=pltpu.SMEM)] + [vmem] * (len(args) - 1)
    args = [args[0]] + [pltpu.with_memory_space_constraint(a, pltpu.VMEM) for a in args[1:]]
    held = pltpu.VMEM if keep else jax.ShapeDtypeStruct
    outs = pl.pallas_call(
        kernel,
        out_shape=[held(shape, jnp.float32) for shape in shapes],
        in_specs=specs,
        out_specs=[vmem] * len(shapes),
        scratch_shapes=list(scratch_shapes),
        input_output_aliases=aliases or {},
        cost_estimate=pl.CostEstimate(flops=flops, bytes_accessed=10**6, transcendentals=0),
        compiler_params=pltpu.CompilerParams(vmem_limit_bytes=24 * 2**20),
    )(*args)
    return outs if len(shapes) > 1 else outs[0]


def first_call(place, chunk, field, mask, link, speed, matrix, dtau):
    vmem = pl.BlockSpec(memory_space=pltpu.VMEM)
    nj, ni = mask.shape[1:]
    given = (field, mask, link, speed, matrix, dtau)
    sources = [pltpu.with_memory_space_constraint(a, pltpu.HBM) for a in given]
    outs = [pltpu.VMEM(a.shape, a.dtype) for a in given]
    outs += [pltpu.VMEM(shape, jnp.float32) for shape in (field.shape, (LIVE, nj, ni))]
    return pl.pallas_call(
        first_kernel,
        out_shape=outs,
        in_specs=[pl.BlockSpec(memory_space=pltpu.SMEM)] * 2 + [pl.BlockSpec(memory_space=pltpu.HBM)] * 6,
        out_specs=[vmem] * 8,
        scratch_shapes=[*scratch(nj, ni), pltpu.SemaphoreType.DMA((6,))],
        cost_estimate=pl.CostEstimate(flops=10**8, bytes_accessed=10**6, transcendentals=0),
        compiler_params=pltpu.CompilerParams(vmem_limit_bytes=24 * 2**20),
    )(place, chunk, *sources)


def shards(head, matrix, state, frame_velocity, dtau, live_mask, link):
    nj, ni = live_mask.shape[1:]
    flaps, gusts = lax.axis_size("flap"), lax.axis_size("gust")
    count = flaps * gusts
    field = state[0, 0]
    first = jnp.where(lax.axis_index("span") == 0, 1, 0).astype(jnp.int32)[None]
    chunk = lax.axis_index("flap") * gusts + lax.axis_index("gust")
    chunk = jnp.where(chunk == 0, head, jnp.where(chunk == head, 0, chunk)).astype(jnp.int32)[None]
    order = headed(count, head)
    swap = [(0, 1), (1, 0)]

    def turn(x):
        y = lax.all_to_all(x.reshape(count, 4, ni), ("flap", "gust"), 0, 0, tiled=True, axis_index_groups=[order])
        return y.reshape(count * 4, ni)

    with jax.named_scope("halo"):
        other = lax.ppermute(field, "span", swap)
    with jax.named_scope("first_divergence"):
        held, mask, link, speed, matrix, dtau, div, near = first_call(
            first, chunk, field, live_mask, link[None], frame_velocity[0], matrix, dtau
        )
        pack = call(first_edge_kernel, [(count * 4, ni)], (first, speed, near, other, held, div))
    with jax.named_scope("turn"):
        pack = turn(pack)
    with jax.named_scope("instances"):
        pack = call(instances_kernel, [pack.shape], (chunk, matrix, pack, dtau, mask), (), 10**8)
    with jax.named_scope("turn_back"):
        pack = turn(pack)
    with jax.named_scope("halo"):
        other = lax.ppermute(call(edge_kernel, [(5, nj, ni)], (first, pack)), "span", swap)
    with jax.named_scope("last_divergence"):
        most, near = call(
            last_kernel,
            [field.shape, (LIVE, nj, ni)],
            (first, speed, pack, mask, dtau, link),
            scratch(nj, ni),
            10**8,
        )
        out = call(last_edge_kernel, [field.shape], (first, speed, near, other, most, mask, dtau), keep=False)
    return out[None, None]


def headed(count, head):
    order = list(range(count))
    order[0], order[head] = head, 0
    return order


def solution(mesh):
    flap = instance_matrix(mesh.shape["flap"], FLAP_OMEGA)
    gust = instance_matrix(mesh.shape["gust"], GUST_OMEGA)
    matrix = np.kron(flap, np.eye(len(gust))) + np.kron(np.eye(len(flap)), gust)
    head = HEAD_FLAP * len(gust) + HEAD_GUST
    order = headed(len(matrix), head)
    matrix = jnp.asarray(matrix[order][:, order].astype(np.float32))
    in_specs = (
        P("flap", "gust", None, "span", None, None),
        P("flap", "gust", None),
        P("span", None, None),
        P("span", None, None),
        P(),
    )
    out_specs = P("flap", "gust", None, "span", None, None)
    return jax.shard_map(
        functools.partial(shards, head, matrix), mesh=mesh, in_specs=in_specs, out_specs=out_specs, check_vma=False
    )
```
